128 devices in a mesh: dp: 16 (over y_lo, x, core), mp: 8 (over z, y_hi).
Axes of the slice: x: 4, y: 4 (y_hi: 2, y_lo: 2; y = y_hi * 2 + y_lo), z: 4, core: 2. Of those that a mesh axis runs over, the one named last changes fastest.
Arguments:
- tokens: bfloat16 [128, 98304], P('dp', 'mp'), may hold values from -6 to 6
- norm_gain: float32 [1536], replicated, may hold values from 0.25 to 1.75
- qkv_weight: bfloat16 [3, 1536, 1536], P(None, 'mp'), may hold values from -0.15625 to 0.15625
- out_weight: bfloat16 [1536, 1536], P('mp'), may hold values from -0.15625 to 0.15625
- text_embed: bfloat16 [128, 1536], P(('dp', 'mp')), may hold values from -0.1875 to 0.1875
- log_temp: float32 [1], replicated, may hold values from 0.5 to 1.5
- logit_bias: float32 [1], replicated, may hold values from -3 to -1
Outputs:
- text_grad: float32 [128, 1536], P(('dp', 'mp'))
- qkv_grad: float32 [3, 1536, 1536], P(None, 'mp', 'dp')
- out_grad: float32 [1536, 1536], P('mp', 'dp')
The draws below stay inside these ranges and needn't reach their ends.
All inputs are finite; a program needn't handle non-finite values.
Results may differ from the reference program's by a relative error of at most 0.03.
Values may be sent and summed in bfloat16 or wider, within the bound.
No kernel may reach another device: no remote copies, remote signals or barrier semaphores. Data moves between devices by JAX's collectives and lax.ppermute only.
A program may use at most 64 MiB of HBM per device.

```python
import math
import jax
import jax.numpy as jnp
from jax import lax

D = 1536
H = 16
DH = 96
P_SIZE = 64
IMG_DEV = 8
HD = 1536
IMAGES = 128


def block_levels(own_key, shape, shards, low, high):
    factor_of = 1.0
    for position, blocks in shards:
        draws = jax.random.uniform(jax.random.fold_in(jax.random.fold_in(own_key, 6), position), (blocks,), jnp.float32, low / len(shards), high / len(shards))
        factor_of = factor_of * jnp.repeat(jnp.exp(draws), shape[position] // blocks).reshape((-1,) + (1,) * (len(shape) - 1 - position))
    return factor_of


def scatter_about(stream_key, dims, scale, bound, shards=(), kind=jnp.bfloat16):
    entries = jax.random.normal(stream_key, dims, jnp.float32) * scale
    if len(shards) > 0:
        entries = block_levels(stream_key, dims, shards, -0.22, 0.18) * entries
    return jnp.clip(entries, min=-bound, max=bound).astype(kind)


def setup_inputs(seed: int = 0) -> dict:
    seeds = jax.random.split(jax.random.key(seed), 8)
    return {
        "tokens": scatter_about(seeds[0], (IMAGES, P_SIZE * D), 1.0, 6.0, ((0, 16), (1, 8))),
        "norm_gain": jnp.clip(1.0 + 0.15 * jax.random.normal(seeds[1], (D,), jnp.float32), 0.25, 1.75),
        "qkv_weight": scatter_about(seeds[2], (3, HD, D), D ** -0.5, 0.15625, ((1, 8),)),
        "out_weight": scatter_about(seeds[3], (HD, D), HD ** -0.5, 0.15625, ((0, 8),)),
        "text_embed": scatter_about(seeds[4], (IMAGES, D), 0.03, 0.1875, ((0, 128),)),
        "log_temp": jnp.clip(jax.random.uniform(seeds[5], (1,), jnp.float32, 0.5, 1.5), 0.5, 1.5),
        "logit_bias": jnp.clip(jax.random.uniform(seeds[6], (1,), jnp.float32, -3.0, -1.0), -3.0, -1.0),
    }


EPS = 1e-06

def layer_norm(block, norm_gain):
    values = block.astype(jnp.float32)
    center = values - lax.optimization_barrier(jnp.mean(values, axis=-1, keepdims=True))
    spread = lax.optimization_barrier(jnp.mean(center * center, axis=-1, keepdims=True))
    return (values, (center * lax.rsqrt(spread + EPS) * norm_gain).astype(jnp.bfloat16))

def forward_block(block, norm_gain, qkv_weight, head_size):
    values, normed = layer_norm(block, norm_gain)
    count, length = (block.shape[0], block.shape[1])
    width = qkv_weight.shape[1]
    mixed = jnp.einsum('bpd,cfd->bpcf', normed.astype(jnp.float32), qkv_weight.astype(jnp.float32)).astype(jnp.bfloat16)
    shaped = mixed.reshape(count, length, 3, width // head_size, head_size)
    query_rows, key_rows, value_rows = (shaped[:, :, 0], shaped[:, :, 1], shaped[:, :, 2])
    scores = jnp.einsum('bqhd,bkhd->bhqk', query_rows.astype(jnp.float32), key_rows.astype(jnp.float32)) / math.sqrt(head_size)
    weights = jnp.exp(scores)
    probs = (weights / lax.optimization_barrier(jnp.sum(weights, axis=-1, keepdims=True))).astype(jnp.bfloat16)
    attended = jnp.einsum('bhqk,bkhd->bqhd', probs.astype(jnp.float32), value_rows.astype(jnp.float32)).astype(jnp.bfloat16)
    return (values, normed, query_rows, key_rows, value_rows, probs, attended.reshape(count, length, width))

def reference(tokens, norm_gain, qkv_weight, out_weight, text_embed, log_temp, logit_bias):
    blocks = tokens.reshape(IMAGES // IMG_DEV, IMG_DEV, P_SIZE, D)

    def pool_block(block):
        values, normed, query_rows, key_rows, value_rows, probs, attended = forward_block(block, norm_gain, qkv_weight, DH)
        branch = jnp.einsum('bpf,fd->bpd', attended.astype(jnp.float32), out_weight.astype(jnp.float32))
        return lax.optimization_barrier(jnp.mean(values + branch, axis=1))
    pooled = lax.map(pool_block, blocks).reshape(IMAGES, D)
    scale = jnp.exp(log_temp[0])
    image_inv = lax.rsqrt(lax.optimization_barrier(jnp.sum(pooled * pooled, axis=-1, keepdims=True)) + EPS)
    image_unit = pooled * image_inv
    text_vals = text_embed.astype(jnp.float32)
    text_inv = lax.rsqrt(lax.optimization_barrier(jnp.sum(text_vals * text_vals, axis=-1, keepdims=True)) + EPS)
    text_unit = text_vals * text_inv
    logits = scale * jnp.dot(image_unit, text_unit.T, precision=lax.Precision.HIGHEST) + logit_bias[0]
    pair_grad = jax.nn.sigmoid(logits) - jnp.eye(IMAGES, dtype=jnp.float32)
    text_unit_grad = scale * jnp.dot(pair_grad.T, image_unit, precision=lax.Precision.HIGHEST)
    text_grad = (text_unit_grad - text_unit * lax.optimization_barrier(jnp.sum(text_unit * text_unit_grad, axis=-1, keepdims=True))) * text_inv
    image_unit_grad = scale * jnp.dot(pair_grad, text_unit, precision=lax.Precision.HIGHEST)
    pooled_grad = (image_unit_grad - image_unit * lax.optimization_barrier(jnp.sum(image_unit * image_unit_grad, axis=-1, keepdims=True))) * image_inv
    resid_grad = (pooled_grad / P_SIZE).astype(jnp.bfloat16).reshape(IMAGES // IMG_DEV, IMG_DEV, D)

    def back_block(carry, inputs):
        block, grad_rows = inputs
        qkv_acc, out_acc = carry
        values, normed, query_rows, key_rows, value_rows, probs, attended = forward_block(block, norm_gain, qkv_weight, DH)
        count = block.shape[0]
        out_acc = out_acc + jnp.einsum('bpf,bd->fd', attended.astype(jnp.float32), grad_rows.astype(jnp.float32))
        attend_grad = jnp.dot(grad_rows, out_weight.T, preferred_element_type=jnp.float32).astype(jnp.bfloat16)
        attend_full = jnp.broadcast_to(attend_grad.reshape(count, 1, H, DH), (count, P_SIZE, H, DH)).astype(jnp.float32)
        prob_grad = jnp.einsum('bqhd,bkhd->bhqk', attend_full, value_rows.astype(jnp.float32))
        prob_vals = probs.astype(jnp.float32)
        value_grad = jnp.einsum('bhqk,bqhd->bkhd', prob_vals, attend_full).astype(jnp.bfloat16)
        score_grad = (prob_vals * (prob_grad - lax.optimization_barrier(jnp.sum(prob_vals * prob_grad, axis=-1, keepdims=True))) / math.sqrt(DH)).astype(jnp.bfloat16)
        query_grad = jnp.einsum('bhqk,bkhd->bqhd', score_grad.astype(jnp.float32), key_rows.astype(jnp.float32)).astype(jnp.bfloat16)
        key_grad = jnp.einsum('bhqk,bqhd->bkhd', score_grad.astype(jnp.float32), query_rows.astype(jnp.float32)).astype(jnp.bfloat16)
        stacked = jnp.stack([query_grad, key_grad, value_grad], axis=2).reshape(count, P_SIZE, 3, HD)
        qkv_acc = qkv_acc + jnp.einsum('bpd,bpcf->cfd', normed.astype(jnp.float32), stacked.astype(jnp.float32))
        return ((qkv_acc, out_acc), None)
    start = (jnp.zeros((3, HD, D), jnp.float32), jnp.zeros((HD, D), jnp.float32))
    (qkv_grad, out_grad), unused = lax.scan(back_block, start, (blocks, resid_grad))
    return (text_grad, qkv_grad, out_grad)
```

```python
import math

import jax
import jax.numpy as jnp
from jax import lax
from jax.experimental import pallas as pl
from jax.experimental.pallas import tpu as pltpu
from jax.sharding import PartitionSpec as P

D = 1536
DH = 96
TOK = 64
IMG = 8
MP = 8
DP = 16
TEXT = DP * MP
WIDTH = 192
EPS = 1e-06
F32 = jnp.float32
BF16 = jnp.bfloat16
SCALE = 1.0 / math.sqrt(DH)
ROWS = 400
LAST = (((1,), (1,)), ((), ()))
FIRST = (((0,), (0,)), ((), ()))
PARAMS = pltpu.CompilerParams(vmem_limit_bytes=48 * 1024 * 1024)


def dot(a, b, dims):
    return lax.dot_general(a, b, dims, preferred_element_type=F32)


def pieces(a, n):
    out = []
    for _ in range(n):
        p = a.astype(BF16)
        out.append(p)
        a = a - p.astype(F32)
    return out


def lanes(shape):
    return lax.broadcasted_iota(jnp.int32, shape, len(shape) - 1)


def norm_kernel(tok_ref, gain_ref, text_ref, out_ref, sum_ref, rows_ref):
    gain = gain_ref[...]
    total = jnp.zeros((IMG, D), F32)
    for t in range(8):
        x = tok_ref[:, t * D:(t + 1) * D].astype(F32)
        center = x - jnp.mean(x, axis=-1, keepdims=True)
        spread = jnp.mean(center * center, axis=-1, keepdims=True)
        row = center * lax.rsqrt(spread + EPS) * gain
        for i in range(12):
            rows_ref[pl.ds(i * 64 + t, IMG, stride=8), :] = row[:, i * 128:(i + 1) * 128]
        total = total + x
    sum_ref[...] = total
    normed = jnp.concatenate([rows_ref[i * 64:(i + 1) * 64, :] for i in range(12)], axis=1)
    normed = normed.astype(BF16)
    text = text_ref[...]
    for d in range(MP):
        out_ref[d, 0:64, :] = normed
        out_ref[d, 64:80, :] = text


def forward_kernel(g_ref, w_ref, wo_ref, sum_ref, part_ref, qkv_ref, probs_ref, att_ref, wide_ref):
    normed = g_ref[:, 0:64, :].reshape(512, D)
    for c in range(3):
        wide_ref[...] = dot(normed, w_ref[c], LAST)
        for b in range(IMG):
            block = jnp.concatenate(
                [wide_ref[(s * 8 + b) * 8:(s * 8 + b) * 8 + 8, :] for s in range(MP)], axis=0
            )
            qkv_ref[c, b * 64:(b + 1) * 64, :] = block.astype(BF16)
    lane = lanes((64, WIDTH))
    for b in range(IMG):
        rows = slice(b * 64, (b + 1) * 64)
        q, k = qkv_ref[0, rows, :], qkv_ref[1, rows, :]
        v = qkv_ref[2, rows, :].astype(F32)
        columns = []
        for h in range(2):
            inside = lane < DH if h == 0 else lane >= DH
            score = dot(k, jnp.where(inside, q, jnp.zeros_like(q)), LAST) * SCALE
            weights = jnp.exp(score)
            probs = (weights / jnp.sum(weights, axis=0, keepdims=True)).astype(BF16)
            probs_ref[b * 2 + h] = probs
            columns.append(jnp.sum(probs.astype(F32), axis=1, keepdims=True))
        attended = jnp.sum(jnp.where(lane < DH, columns[0], columns[1]) * v, axis=0, keepdims=True)
        att_ref[b:b + 1, :] = attended
    high, low = pieces(att_ref[...], 2)
    branch = dot(jnp.concatenate([high, low], axis=0), wo_ref[...], (((1,), (0,)), ((), ())))
    part = ((branch[0:8] + branch[8:16] + sum_ref[...]) * (1.0 / TOK)).astype(BF16)
    for d in range(MP):
        part_ref[d] = part


def backward_kernel(
    g_ref, part_ref, qkv_ref, probs_ref, att_ref, wo_ref, temp_ref, bias_ref,
    keep_ref, give_ref, grad_ref, turn_ref, text_ref, both_ref,
):
    me = lax.axis_index("dp")
    slot = lax.axis_index("mp")
    core = lax.rem(me, 2)
    pooled = jnp.zeros((IMG, D), F32)
    for s in range(MP):
        pooled = pooled + part_ref[s].astype(F32)
    scale = jnp.exp(temp_ref[...])
    image_inv = lax.rsqrt(jnp.sum(pooled * pooled, axis=-1, keepdims=True) + EPS)
    unit = pooled * image_inv
    text = g_ref[:, 64:80, :].reshape(TEXT, D)
    wide_text = text.astype(F32)
    square = pieces(wide_text * wide_text, 2)
    ones = jnp.ones((IMG, D), BF16)
    text_inv = lax.rsqrt(dot(ones, square[0], LAST) + dot(ones, square[1], LAST) + EPS)
    cosine = dot(jnp.concatenate(pieces(unit, 3), axis=0), text, LAST)
    cosine = (cosine[0:8] + cosine[8:16] + cosine[16:24]) * text_inv
    logits = scale * cosine + bias_ref[...]
    image_row = lax.broadcasted_iota(jnp.int32, (IMG, TEXT), 0)
    own = lanes((IMG, TEXT)) == image_row * DP + me
    pair = scale * (jax.nn.sigmoid(logits) - jnp.where(own, 1.0, 0.0))
    unit_grad = dot(
        jnp.concatenate(pieces(pair * text_inv, 3), axis=0), text, (((1,), (0,)), ((), ()))
    )
    unit_grad = unit_grad[0:8] + unit_grad[8:16] + unit_grad[16:24]
    pooled_grad = (unit_grad - unit * jnp.sum(unit * unit_grad, axis=-1, keepdims=True)) * image_inv
    resid = (pooled_grad * (1.0 / TOK)).astype(BF16)
    mine = pltpu.roll(pair, lax.rem(TEXT - slot * DP, TEXT), axis=1)
    pair_high, pair_low = pieces(mine, 2)
    unit_high, unit_low = pieces(unit, 2)
    text_grad = dot(
        jnp.concatenate([pair_high, pair_high, pair_low], axis=0),
        jnp.concatenate([unit_high, unit_low, unit_high], axis=0),
        FIRST,
    )
    text_ref[...] = jnp.zeros_like(text_ref)
    for i in range(12):
        text_ref[pl.ds(i, DP, stride=16), :] = text_grad[0:DP, i * 128:(i + 1) * 128]
    attend = dot(resid, wo_ref[...], LAST).astype(BF16)
    wide_attend = attend.astype(F32)
    lane = lanes((64, WIDTH))
    slim = lanes((64, 64))
    for b in range(IMG):
        rows = slice(b * 64, (b + 1) * 64)
        q, k = qkv_ref[0, rows, :], qkv_ref[1, rows, :]
        product = qkv_ref[2, rows, :].astype(F32) * wide_attend[b:b + 1, :]
        query_grad, key_grad, factor = [], [], jnp.zeros((64, 64), F32)
        for h in range(2):
            inside = lane < DH if h == 0 else lane >= DH
            prob_grad = jnp.sum(jnp.where(inside, product, 0.0), axis=1, keepdims=True)
            probs = probs_ref[b * 2 + h].astype(F32)
            mean = jnp.sum(probs * prob_grad, axis=0, keepdims=True)
            score_grad = (probs * (prob_grad - mean) * SCALE).astype(BF16)
            query_grad.append(dot(score_grad, k, FIRST))
            key_grad.append(dot(score_grad, q, (((1,), (0,)), ((), ()))))
            column = jnp.sum(probs, axis=1, keepdims=True)
            factor = factor + jnp.where(slim == h * 8 + b, column, 0.0)
        query_grad = jnp.where(lane < DH, query_grad[0], query_grad[1])
        key_grad = jnp.where(lane < DH, key_grad[0], key_grad[1])
        first = jnp.where(core == 0, factor, 0.0)
        full = jnp.concatenate([query_grad, first, key_grad, factor - first], axis=1)
        for s in range(MP):
            grad_ref[(s * 8 + b) * 8:(s * 8 + b) * 8 + 8, :] = full[s * 8:s * 8 + 8, :]
    turn_ref[...] = jnp.zeros_like(turn_ref)
    start = pl.multiple_of(core * 128, 128)
    for h in range(2):
        part = slice(h * DH, (h + 1) * DH)
        turn_ref[pl.ds(start + 96 + h * 8, 8), 0:DH] = wide_attend[:, part]
        turn_ref[pl.ds(start + 112 + h * 8, 8), 0:DH] = att_ref[:, part]
    turned = [turn_ref[i * 128:(i + 1) * 128, :].T[0:DH, :] for i in range(2)]
    place = lanes((IMG, 512)) - lax.broadcasted_iota(jnp.int32, (IMG, 512), 0) - core * 256
    spot = jnp.where((place == 208) | (place == 216), 1.0, 0.0).astype(BF16)
    normed = g_ref[:, 0:64, :].reshape(512, D)
    grads = grad_ref[...].astype(BF16)
    for c in range(4):
        columns = slice(c * 384, (c + 1) * 384)
        y = dot(normed[:, columns], grads, FIRST) + dot(resid[:, columns], spot, FIRST)
        for j in range(4):
            d = c * 4 + j
            for i in range(4):
                block = y[j * 96:(j + 1) * 96, i * 128:(i + 1) * 128]
                if i % 2 == 1:
                    block = block + turned[i // 2]
                both_ref[d % 2, d // 2, i * 96:(i + 1) * 96, :] = block.astype(BF16)
            both_ref[d % 2, d // 2, 384:400, :] = text_ref[d * 16:(d + 1) * 16, :].astype(BF16)
    keep_ref[...] = both_ref[core]
    give_ref[...] = both_ref[1 - core]


def finish_kernel(r_ref, text_ref, text_out, qkv_out, out_out, stack_ref):
    total = r_ref[0].astype(F32)
    for s in range(1, 8):
        total = total + r_ref[s].astype(F32)
    unit_grad = total[384:396, :]
    text = text_ref[...].astype(F32)
    inv = lax.rsqrt(jnp.sum(text * text, keepdims=True) + EPS)
    unit = text * inv
    text_out[...] = (unit_grad - unit * jnp.sum(unit * unit_grad, keepdims=True)) * inv
    pad = jnp.zeros((32, 128), F32)
    for c in range(2):
        for i in range(2):
            at = (c * 2 + i) * 96
            turned = jnp.concatenate([total[at:at + 96, :], pad], axis=0).T
            rows = 128 if i == 0 else 64
            qkv_out[c, i * 128:i * 128 + rows, :] = turned[0:rows, 0:96]
    lane = lanes((96, 128))
    group = lax.shift_right_logical(lane, 3) - 8
    factors = []
    for s in range(8):
        for c in range(2):
            block = r_ref[s, (c * 2 + 1) * 96:(c * 2 + 2) * 96, :]
            factors.append(block)
            rolled = pltpu.roll(block.astype(F32), 96, axis=1)
            for g in range(4):
                at = (s * 2 + c) * 128
                stack_ref[g * 96:(g + 1) * 96, at:at + 128] = jnp.where(
                    group == g, rolled, 0.0
                ).astype(BF16)
    product = dot(stack_ref[...], jnp.concatenate(factors, axis=1), LAST)
    qkv_out[2] = product[0:192, :]
    out_out[...] = product[192:384, :]


def call(kernel, outs, scratch, *args):
    return pl.pallas_call(
        kernel,
        out_shape=[jax.ShapeDtypeStruct(*o) for o in outs],
        scratch_shapes=[pltpu.VMEM(*s) for s in scratch],
        compiler_params=PARAMS,
    )(*args)


def body(tokens, norm_gain, qkv_weight, out_weight, text_embed, log_temp, logit_bias):
    texts = lax.all_to_all(
        jnp.broadcast_to(text_embed[None], (DP, 1, D)), "dp", 0, 0
    ).reshape(DP, D)
    copies, token_sum = call(
        norm_kernel,
        [((MP, 80, D), BF16), ((IMG, D), F32)],
        [((12 * 64, 128), F32)],
        tokens, norm_gain.reshape(1, D), texts,
    )
    gathered = lax.all_to_all(copies, "mp", 0, 0)
    part, qkv, probs, attended = call(
        forward_kernel,
        [((MP, IMG, D), BF16), ((3, 512, WIDTH), BF16), ((16, 64, 64), BF16), ((IMG, WIDTH), F32)],
        [((512, WIDTH), F32)],
        gathered, qkv_weight, out_weight, token_sum,
    )
    parts = lax.all_to_all(part, "mp", 0, 0)
    keep, give = call(
        backward_kernel,
        [((8, ROWS, 128), BF16)] * 2,
        [((512, 512), F32), ((256, 128), F32), ((256, 128), F32), ((2, 8, ROWS, 128), BF16)],
        gathered, parts, qkv, probs, attended, out_weight,
        log_temp.reshape(1, 1), logit_bias.reshape(1, 1),
    )
    other = lax.ppermute(give, "dp", [(i, i ^ 1) for i in range(DP)])
    send = (keep.astype(F32) + other.astype(F32)).astype(BF16)
    received = lax.all_to_all(
        send, "dp", 0, 0, axis_index_groups=[list(range(c, DP, 2)) for c in range(2)]
    )
    text_grad, qkv_grad, out_grad = call(
        finish_kernel,
        [((12, 128), F32), ((3, WIDTH, 96), F32), ((WIDTH, 96), F32)],
        [((384, 2048), BF16)],
        received, text_embed.reshape(12, 128),
    )
    return (text_grad.reshape(1, D), qkv_grad, out_grad)


def solution(mesh):
    placed = (
        P("dp", "mp"),
        P(),
        P(None, "mp", None),
        P("mp", None),
        P(("dp", "mp"), None),
        P(),
        P(),
    )
    return jax.shard_map(
        body,
        mesh=mesh,
        in_specs=placed,
        out_specs=(P(("dp", "mp"), None), P(None, "mp", "dp"), P("mp", "dp")),
        check_vma=False,
    )
```

```python
import math

import jax
import jax.numpy as jnp
from jax import lax
from jax.experimental import pallas as pl
from jax.experimental.pallas import tpu as pltpu
from jax.sharding import PartitionSpec as P

D = 1536
DH = 96
TOK = 64
IMG = 8
MP = 8
DP = 16
TEXT = DP * MP
WIDTH = 192
EPS = 1e-06
F32 = jnp.float32
BF16 = jnp.bfloat16
SCALE = 1.0 / math.sqrt(DH)
ROWS = 400
LAST = (((1,), (1,)), ((), ()))
FIRST = (((0,), (0,)), ((), ()))
PARAMS = pltpu.CompilerParams(vmem_limit_bytes=48 * 1024 * 1024)


def dot(a, b, dims):
    return lax.dot_general(a, b, dims, preferred_element_type=F32)


def pieces(a, n):
    out = []
    for _ in range(n):
        p = a.astype(BF16)
        out.append(p)
        a = a - p.astype(F32)
    return out


def lanes(shape):
    return lax.broadcasted_iota(jnp.int32, shape, len(shape) - 1)


def norm_kernel(tok_ref, gain_ref, text_ref, out_ref, sum_ref, text_out, rows_ref, line_ref):
    total = jnp.zeros((IMG, D), F32)
    for t in range(8):
        x = tok_ref[:, t * D:(t + 1) * D].astype(F32)
        center = x - jnp.mean(x, axis=-1, keepdims=True)
        spread = jnp.mean(center * center, axis=-1, keepdims=True)
        row = center * lax.rsqrt(spread + EPS)
        for i in range(12):
            rows_ref[pl.ds(i * 64 + t, IMG, stride=8), :] = (
                row[:, i * 128:(i + 1) * 128] * gain_ref[i:i + 1, :]
            )
        total = total + x
    sum_ref[...] = total
    out_ref[...] = jnp.concatenate(
        [rows_ref[i * 64:(i + 1) * 64, :] for i in range(12)], axis=1
    ).astype(BF16)
    line_ref[...] = jnp.zeros_like(line_ref)
    for i in range(12):
        line_ref[i:i + 1, :] = text_ref[:, i * 128:(i + 1) * 128].astype(F32)
    line = line_ref[...].astype(BF16)
    for d in range(DP):
        text_out[d] = line


def forward_kernel(*refs):
    shards, (w_ref, wo_ref, sum_ref, text_ref), refs = refs[:MP], refs[MP:MP + 4], refs[MP + 4:]
    part_ref, qkv_ref, probs_ref, att_ref, wide_ref, line_ref = refs
    normed = jnp.concatenate([r[...] for r in shards], axis=0)
    for c in range(3):
        wide_ref[...] = dot(normed, w_ref[c], LAST)
        for b in range(IMG):
            block = jnp.concatenate(
                [wide_ref[(s * 8 + b) * 8:(s * 8 + b) * 8 + 8, :] for s in range(MP)], axis=0
            )
            qkv_ref[c, b * 64:(b + 1) * 64, :] = block.astype(BF16)
    lane = lanes((64, WIDTH))
    for b in range(IMG):
        rows = slice(b * 64, (b + 1) * 64)
        q, k = qkv_ref[0, rows, :], qkv_ref[1, rows, :]
        v = qkv_ref[2, rows, :].astype(F32)
        columns = []
        for h in range(2):
            inside = lane < DH if h == 0 else lane >= DH
            score = dot(k, jnp.where(inside, q, jnp.zeros_like(q)), LAST) * SCALE
            weights = jnp.exp(score)
            probs = (weights / jnp.sum(weights, axis=0, keepdims=True)).astype(BF16)
            probs_ref[b * 2 + h] = probs
            columns.append(jnp.sum(probs.astype(F32), axis=1, keepdims=True))
        attended = jnp.sum(jnp.where(lane < DH, columns[0], columns[1]) * v, axis=0, keepdims=True)
        att_ref[b:b + 1, :] = attended
    high, low = pieces(att_ref[...], 2)
    branch = dot(jnp.concatenate([high, low], axis=0), wo_ref[...], (((1,), (0,)), ((), ())))
    part = ((branch[0:8] + branch[8:16] + sum_ref[...]) * (1.0 / TOK)).astype(BF16)
    line_ref[...] = text_ref[...].astype(F32).reshape(DP * 16, 128)
    texts = jnp.concatenate(
        [line_ref[pl.ds(i, DP, stride=16), :] for i in range(12)], axis=1
    ).astype(BF16)
    for d in range(MP):
        part_ref[d, 0:16, :] = texts
        part_ref[d, 16:24, :] = part


def backward_kernel(*refs):
    shards, refs = refs[:MP], refs[MP:]
    part_ref, qkv_ref, probs_ref, att_ref, wo_ref, temp_ref, bias_ref = refs[:7]
    keep_ref, give_ref, grad_ref, turn_ref, text_ref, both_ref = refs[7:]
    me = lax.axis_index("dp")
    slot = lax.axis_index("mp")
    core = lax.rem(me, 2)
    pooled = jnp.zeros((IMG, D), F32)
    for s in range(MP):
        pooled = pooled + part_ref[s, 16:24, :].astype(F32)
    scale = jnp.exp(temp_ref[...])
    image_inv = lax.rsqrt(jnp.sum(pooled * pooled, axis=-1, keepdims=True) + EPS)
    unit = pooled * image_inv
    text = part_ref[:, 0:16, :].reshape(TEXT, D)
    wide_text = text.astype(F32)
    square = pieces(wide_text * wide_text, 2)
    ones = jnp.ones((IMG, D), BF16)
    text_inv = lax.rsqrt(dot(ones, square[0], LAST) + dot(ones, square[1], LAST) + EPS)
    cosine = dot(jnp.concatenate(pieces(unit, 3), axis=0), text, LAST)
    cosine = (cosine[0:8] + cosine[8:16] + cosine[16:24]) * text_inv
    logits = scale * cosine + bias_ref[...]
    image_row = lax.broadcasted_iota(jnp.int32, (IMG, TEXT), 0)
    own = lanes((IMG, TEXT)) == image_row * DP + me
    pair = scale * (jax.nn.sigmoid(logits) - jnp.where(own, 1.0, 0.0))
    unit_grad = dot(
        jnp.concatenate(pieces(pair * text_inv, 3), axis=0), text, (((1,), (0,)), ((), ()))
    )
    unit_grad = unit_grad[0:8] + unit_grad[8:16] + unit_grad[16:24]
    pooled_grad = (unit_grad - unit * jnp.sum(unit * unit_grad, axis=-1, keepdims=True)) * image_inv
    resid = (pooled_grad * (1.0 / TOK)).astype(BF16)
    mine = pltpu.roll(pair, lax.rem(TEXT - slot * DP, TEXT), axis=1)
    pair_high, pair_low = pieces(mine, 2)
    unit_high, unit_low = pieces(unit, 2)
    text_grad = dot(
        jnp.concatenate([pair_high, pair_high, pair_low], axis=0),
        jnp.concatenate([unit_high, unit_low, unit_high], axis=0),
        FIRST,
    )
    text_ref[...] = jnp.zeros_like(text_ref)
    for i in range(12):
        text_ref[pl.ds(i, DP, stride=16), :] = text_grad[0:DP, i * 128:(i + 1) * 128]
    attend = dot(resid, wo_ref[...], LAST).astype(BF16)
    wide_attend = attend.astype(F32)
    lane = lanes((64, WIDTH))
    slim = lanes((64, 64))
    for b in range(IMG):
        rows = slice(b * 64, (b + 1) * 64)
        q, k = qkv_ref[0, rows, :], qkv_ref[1, rows, :]
        product = qkv_ref[2, rows, :].astype(F32) * wide_attend[b:b + 1, :]
        query_grad, key_grad, factor = [], [], jnp.zeros((64, 64), F32)
        for h in range(2):
            inside = lane < DH if h == 0 else lane >= DH
            prob_grad = jnp.sum(jnp.where(inside, product, 0.0), axis=1, keepdims=True)
            probs = probs_ref[b * 2 + h].astype(F32)
            mean = jnp.sum(probs * prob_grad, axis=0, keepdims=True)
            score_grad = (probs * (prob_grad - mean) * SCALE).astype(BF16)
            query_grad.append(dot(score_grad, k, FIRST))
            key_grad.append(dot(score_grad, q, (((1,), (0,)), ((), ()))))
            column = jnp.sum(probs, axis=1, keepdims=True)
            factor = factor + jnp.where(slim == h * 8 + b, column, 0.0)
        query_grad = jnp.where(lane < DH, query_grad[0], query_grad[1])
        key_grad = jnp.where(lane < DH, key_grad[0], key_grad[1])
        first = jnp.where(core == 0, factor, 0.0)
        full = jnp.concatenate([query_grad, first, key_grad, factor - first], axis=1)
        for s in range(MP):
            grad_ref[(s * 8 + b) * 8:(s * 8 + b) * 8 + 8, :] = full[s * 8:s * 8 + 8, :]
    turn_ref[...] = jnp.zeros_like(turn_ref)
    start = pl.multiple_of(core * 128, 128)
    for h in range(2):
        part = slice(h * DH, (h + 1) * DH)
        turn_ref[pl.ds(start + 96 + h * 8, 8), 0:DH] = wide_attend[:, part]
        turn_ref[pl.ds(start + 112 + h * 8, 8), 0:DH] = att_ref[:, part]
    turned = [turn_ref[i * 128:(i + 1) * 128, :].T[0:DH, :] for i in range(2)]
    place = lanes((IMG, 512)) - lax.broadcasted_iota(jnp.int32, (IMG, 512), 0) - core * 256
    spot = jnp.where((place == 208) | (place == 216), 1.0, 0.0).astype(BF16)
    normed = jnp.concatenate([r[...] for r in shards], axis=0)
    grads = grad_ref[...].astype(BF16)
    for c in range(4):
        columns = slice(c * 384, (c + 1) * 384)
        y = dot(normed[:, columns], grads, FIRST) + dot(resid[:, columns], spot, FIRST)
        for j in range(4):
            d = c * 4 + j
            for i in range(4):
                block = y[j * 96:(j + 1) * 96, i * 128:(i + 1) * 128]
                if i % 2 == 1:
                    block = block + turned[i // 2]
                both_ref[d % 2, d // 2, i * 96:(i + 1) * 96, :] = block.astype(BF16)
            both_ref[d % 2, d // 2, 384:400, :] = text_ref[d * 16:(d + 1) * 16, :].astype(BF16)
    keep_ref[...] = both_ref[core]
    give_ref[...] = both_ref[1 - core]


def finish_kernel(r_ref, text_ref, text_out, qkv_out, out_out, stack_ref, line_ref):
    total = r_ref[0].astype(F32)
    for s in range(1, 8):
        total = total + r_ref[s].astype(F32)
    unit_grad = total[384:396, :]
    for i in range(12):
        line_ref[i:i + 1, :] = text_ref[:, i * 128:(i + 1) * 128].astype(F32)
    text = line_ref[...]
    inv = lax.rsqrt(jnp.sum(text * text, keepdims=True) + EPS)
    unit = text * inv
    line_ref[...] = (unit_grad - unit * jnp.sum(unit * unit_grad, keepdims=True)) * inv
    for i in range(12):
        text_out[:, i * 128:(i + 1) * 128] = line_ref[i:i + 1, :]
    pad = jnp.zeros((32, 128), F32)
    for c in range(2):
        for i in range(2):
            at = (c * 2 + i) * 96
            turned = jnp.concatenate([total[at:at + 96, :], pad], axis=0).T
            rows = 128 if i == 0 else 64
            qkv_out[c, i * 128:i * 128 + rows, :] = turned[0:rows, 0:96]
    lane = lanes((96, 128))
    group = lax.shift_right_logical(lane, 3) - 8
    factors = []
    for s in range(8):
        for c in range(2):
            block = r_ref[s, (c * 2 + 1) * 96:(c * 2 + 2) * 96, :]
            factors.append(block)
            rolled = pltpu.roll(block.astype(F32), 96, axis=1)
            for g in range(4):
                at = (s * 2 + c) * 128
                stack_ref[g * 96:(g + 1) * 96, at:at + 128] = jnp.where(
                    group == g, rolled, 0.0
                ).astype(BF16)
    product = dot(stack_ref[...], jnp.concatenate(factors, axis=1), LAST)
    qkv_out[2] = product[0:192, :]
    out_out[...] = product[192:384, :]


def call(kernel, outs, scratch, *args):
    return pl.pallas_call(
        kernel,
        out_shape=[jax.ShapeDtypeStruct(*o) for o in outs],
        scratch_shapes=[pltpu.VMEM(*s) for s in scratch],
        compiler_params=PARAMS,
    )(*args)


def over_mp(block, dz, dy):
    route = [(i, ((i // 2 + dz) % 4) * 2 + (i % 2 + dy) % 2) for i in range(MP)]
    return lax.ppermute(block, "mp", route)


def body(tokens, norm_gain, qkv_weight, out_weight, text_embed, log_temp, logit_bias):
    own, token_sum, text_copies = call(
        norm_kernel,
        [((64, D), BF16), ((IMG, D), F32), ((DP, 16, 128), BF16)],
        [((12 * 64, 128), F32), ((16, 128), F32)],
        tokens, norm_gain.reshape(12, 128), text_embed,
    )
    across = over_mp(own, 0, 1)
    ahead = over_mp(own, 1, 0)
    behind = over_mp(own, 3, 0)
    far = over_mp(own, 2, 0)
    texts = lax.all_to_all(text_copies, "dp", 0, 0)
    shards = [
        own, across, ahead, behind, far,
        over_mp(across, 1, 0), over_mp(across, 3, 0), over_mp(far, 0, 1),
    ]
    part, qkv, probs, attended = call(
        forward_kernel,
        [((MP, 24, D), BF16), ((3, 512, WIDTH), BF16), ((16, 64, 64), BF16), ((IMG, WIDTH), F32)],
        [((512, WIDTH), F32), ((DP * 16, 128), F32)],
        *shards, qkv_weight, out_weight, token_sum, texts,
    )
    parts = lax.all_to_all(part, "mp", 0, 0)
    keep, give = call(
        backward_kernel,
        [((8, ROWS, 128), BF16)] * 2,
        [((512, 512), F32), ((256, 128), F32), ((256, 128), F32), ((2, 8, ROWS, 128), BF16)],
        *shards, parts, qkv, probs, attended, out_weight,
        log_temp.reshape(1, 1), logit_bias.reshape(1, 1),
    )
    other = lax.ppermute(give, "dp", [(i, i ^ 1) for i in range(DP)])
    send = (keep.astype(F32) + other.astype(F32)).astype(BF16)
    received = lax.all_to_all(
        send, "dp", 0, 0, axis_index_groups=[list(range(c, DP, 2)) for c in range(2)]
    )
    text_grad, qkv_grad, out_grad = call(
        finish_kernel,
        [((1, D), F32), ((3, WIDTH, 96), F32), ((WIDTH, 96), F32)],
        [((384, 2048), BF16), ((12, 128), F32)],
        received, text_embed,
    )
    return (text_grad, qkv_grad, out_grad)


def solution(mesh):
    placed = (
        P("dp", "mp"),
        P(),
        P(None, "mp", None),
        P("mp", None),
        P(("dp", "mp"), None),
        P(),
        P(),
    )
    return jax.shard_map(
        body,
        mesh=mesh,
        in_specs=placed,
        out_specs=(P(("dp", "mp"), None), P(None, "mp", "dp"), P("mp", "dp")),
        check_vma=False,
    )
```

```python
import math

import jax
import jax.numpy as jnp
from jax import lax
from jax.experimental import pallas as pl
from jax.experimental.pallas import tpu as pltpu
from jax.sharding import PartitionSpec as P

D = 1536
DH = 96
TOK = 64
IMG = 8
MP = 8
DP = 16
TEXT = DP * MP
WIDTH = 192
EPS = 1e-06
F32 = jnp.float32
BF16 = jnp.bfloat16
SCALE = 1.0 / math.sqrt(DH)
ROWS = 400
LAST = (((1,), (1,)), ((), ()))
FIRST = (((0,), (0,)), ((), ()))
FULL = 48 * 1024 * 1024
PARAMS = pltpu.CompilerParams(vmem_limit_bytes=48 * 1024 * 1024)


def dot(a, b, dims):
    return lax.dot_general(a, b, dims, preferred_element_type=F32)


def pieces(a, n):
    out = []
    for _ in range(n):
        p = a.astype(BF16)
        out.append(p)
        a = a - p.astype(F32)
    return out


def lanes(shape):
    return lax.broadcasted_iota(jnp.int32, shape, len(shape) - 1)


def line_kernel(text_ref, out_ref, line_ref):
    line_ref[...] = jnp.zeros_like(line_ref)
    for i in range(12):
        line_ref[i:i + 1, :] = text_ref[:, i * 128:(i + 1) * 128].astype(F32)
    line = line_ref[...].astype(BF16)
    for d in range(DP):
        out_ref[d] = line


def norm_kernel(tok_ref, gain_ref, out_ref, sum_ref, rows_ref):
    total = jnp.zeros((IMG, D), F32)
    for t in range(8):
        x = tok_ref[:, t * D:(t + 1) * D].astype(F32)
        center = x - jnp.mean(x, axis=-1, keepdims=True)
        spread = jnp.mean(center * center, axis=-1, keepdims=True)
        row = center * lax.rsqrt(spread + EPS)
        for i in range(12):
            rows_ref[pl.ds(i * 64 + t, IMG, stride=8), :] = (
                row[:, i * 128:(i + 1) * 128] * gain_ref[i:i + 1, :]
            )
        total = total + x
    sum_ref[...] = total
    out_ref[...] = jnp.concatenate(
        [rows_ref[i * 64:(i + 1) * 64, :] for i in range(12)], axis=1
    ).astype(BF16)


def forward_kernel(*refs):
    shards, (w_ref, wo_ref, sum_ref, temp_ref, bias_ref), refs = refs[:MP], refs[MP:MP + 5], refs[MP + 5:]
    part_ref, qkv_ref, probs_ref, att_ref, scalar_ref, wide_ref = refs
    scalar_ref[0:1, :] = jnp.exp(jnp.full((1, 128), temp_ref[0], F32))
    scalar_ref[1:2, :] = jnp.full((1, 128), bias_ref[0], F32)
    normed = jnp.concatenate([r[...] for r in shards], axis=0)
    for c in range(3):
        wide_ref[...] = dot(normed, w_ref[c], LAST)
        for b in range(IMG):
            block = jnp.concatenate(
                [wide_ref[(s * 8 + b) * 8:(s * 8 + b) * 8 + 8, :] for s in range(MP)], axis=0
            )
            qkv_ref[c, b * 64:(b + 1) * 64, :] = block.astype(BF16)
    lane = lanes((64, WIDTH))
    for b in range(IMG):
        rows = slice(b * 64, (b + 1) * 64)
        q, k = qkv_ref[0, rows, :], qkv_ref[1, rows, :]
        v = qkv_ref[2, rows, :].astype(F32)
        columns = []
        for h in range(2):
            inside = lane < DH if h == 0 else lane >= DH
            score = dot(k, jnp.where(inside, q, jnp.zeros_like(q)), LAST) * SCALE
            weights = jnp.exp(score)
            probs = (weights / jnp.sum(weights, axis=0, keepdims=True)).astype(BF16)
            probs_ref[b * 2 + h] = probs
            columns.append(jnp.sum(probs.astype(F32), axis=1, keepdims=True))
        attended = jnp.sum(jnp.where(lane < DH, columns[0], columns[1]) * v, axis=0, keepdims=True)
        att_ref[b:b + 1, :] = attended
    high, low = pieces(att_ref[...], 2)
    branch = dot(jnp.concatenate([high, low], axis=0), wo_ref[...], (((1,), (0,)), ((), ())))
    part = ((branch[0:8] + branch[8:16] + sum_ref[...]) * (1.0 / TOK)).astype(BF16)
    part_ref[...] = part


def join_kernel(part_ref, text_ref, out_ref, line_ref):
    line_ref[...] = text_ref[...].astype(F32).reshape(DP * 16, 128)
    texts = jnp.concatenate(
        [line_ref[pl.ds(i, DP, stride=16), :] for i in range(12)], axis=1
    ).astype(BF16)
    part = part_ref[...]
    for d in range(MP):
        out_ref[d, 0:16, :] = texts
        out_ref[d, 16:24, :] = part


def backward_kernel(*refs):
    shards, refs = refs[:MP], refs[MP:]
    part_ref, qkv_ref, probs_ref, att_ref, scalar_ref, wo_ref = refs[:6]
    keep_ref, give_ref, grad_ref, turn_ref, text_ref, both_ref = refs[6:]
    me = lax.axis_index("dp")
    slot = lax.axis_index("mp")
    core = lax.rem(me, 2)
    pooled = jnp.zeros((IMG, D), F32)
    for s in range(MP):
        pooled = pooled + part_ref[s, 16:24, :].astype(F32)
    scale = scalar_ref[0:1, :]
    image_inv = lax.rsqrt(jnp.sum(pooled * pooled, axis=-1, keepdims=True) + EPS)
    unit = pooled * image_inv
    text = part_ref[:, 0:16, :].reshape(TEXT, D)
    wide_text = text.astype(F32)
    square = pieces(wide_text * wide_text, 2)
    ones = jnp.ones((IMG, D), BF16)
    text_inv = lax.rsqrt(dot(ones, square[0], LAST) + dot(ones, square[1], LAST) + EPS)
    cosine = dot(jnp.concatenate(pieces(unit, 3), axis=0), text, LAST)
    cosine = (cosine[0:8] + cosine[8:16] + cosine[16:24]) * text_inv
    logits = scale * cosine + scalar_ref[1:2, :]
    image_row = lax.broadcasted_iota(jnp.int32, (IMG, TEXT), 0)
    own = lanes((IMG, TEXT)) == image_row * DP + me
    pair = scale * (jax.nn.sigmoid(logits) - jnp.where(own, 1.0, 0.0))
    unit_grad = dot(
        jnp.concatenate(pieces(pair * text_inv, 3), axis=0), text, (((1,), (0,)), ((), ()))
    )
    unit_grad = unit_grad[0:8] + unit_grad[8:16] + unit_grad[16:24]
    pooled_grad = (unit_grad - unit * jnp.sum(unit * unit_grad, axis=-1, keepdims=True)) * image_inv
    resid = (pooled_grad * (1.0 / TOK)).astype(BF16)
    mine = pltpu.roll(pair, lax.rem(TEXT - slot * DP, TEXT), axis=1)
    pair_high, pair_low = pieces(mine, 2)
    unit_high, unit_low = pieces(unit, 2)
    text_grad = dot(
        jnp.concatenate([pair_high, pair_high, pair_low], axis=0),
        jnp.concatenate([unit_high, unit_low, unit_high], axis=0),
        FIRST,
    )
    text_ref[...] = jnp.zeros_like(text_ref)
    for i in range(12):
        text_ref[pl.ds(i, DP, stride=16), :] = text_grad[0:DP, i * 128:(i + 1) * 128]
    attend = dot(resid, wo_ref[...], LAST).astype(BF16)
    wide_attend = attend.astype(F32)
    lane = lanes((64, WIDTH))
    slim = lanes((64, 64))
    for b in range(IMG):
        rows = slice(b * 64, (b + 1) * 64)
        q, k = qkv_ref[0, rows, :], qkv_ref[1, rows, :]
        product = qkv_ref[2, rows, :].astype(F32) * wide_attend[b:b + 1, :]
        query_grad, key_grad, factor = [], [], jnp.zeros((64, 64), F32)
        for h in range(2):
            inside = lane < DH if h == 0 else lane >= DH
            prob_grad = jnp.sum(jnp.where(inside, product, 0.0), axis=1, keepdims=True)
            probs = probs_ref[b * 2 + h].astype(F32)
            mean = jnp.sum(probs * prob_grad, axis=0, keepdims=True)
            score_grad = (probs * (prob_grad - mean) * SCALE).astype(BF16)
            query_grad.append(dot(score_grad, k, FIRST))
            key_grad.append(dot(score_grad, q, (((1,), (0,)), ((), ()))))
            column = jnp.sum(probs, axis=1, keepdims=True)
            factor = factor + jnp.where(slim == h * 8 + b, column, 0.0)
        query_grad = jnp.where(lane < DH, query_grad[0], query_grad[1])
        key_grad = jnp.where(lane < DH, key_grad[0], key_grad[1])
        first = jnp.where(core == 0, factor, 0.0)
        full = jnp.concatenate([query_grad, first, key_grad, factor - first], axis=1)
        for s in range(MP):
            grad_ref[(s * 8 + b) * 8:(s * 8 + b) * 8 + 8, :] = full[s * 8:s * 8 + 8, :]
    turn_ref[...] = jnp.zeros_like(turn_ref)
    start = pl.multiple_of(core * 128, 128)
    for h in range(2):
        part = slice(h * DH, (h + 1) * DH)
        turn_ref[pl.ds(start + 96 + h * 8, 8), 0:DH] = wide_attend[:, part]
        turn_ref[pl.ds(start + 112 + h * 8, 8), 0:DH] = att_ref[:, part]
    turned = [turn_ref[i * 128:(i + 1) * 128, :].T[0:DH, :] for i in range(2)]
    place = lanes((IMG, 512)) - lax.broadcasted_iota(jnp.int32, (IMG, 512), 0) - core * 256
    spot = jnp.where((place == 208) | (place == 216), 1.0, 0.0).astype(BF16)
    normed = jnp.concatenate([r[...] for r in shards], axis=0)
    grads = grad_ref[...].astype(BF16)
    for c in range(4):
        columns = slice(c * 384, (c + 1) * 384)
        y = dot(normed[:, columns], grads, FIRST) + dot(resid[:, columns], spot, FIRST)
        for j in range(4):
            d = c * 4 + j
            for i in range(4):
                block = y[j * 96:(j + 1) * 96, i * 128:(i + 1) * 128]
                if i % 2 == 1:
                    block = block + turned[i // 2]
                both_ref[d % 2, d // 2, i * 96:(i + 1) * 96, :] = block.astype(BF16)
            both_ref[d % 2, d // 2, 384:400, :] = text_ref[d * 16:(d + 1) * 16, :].astype(BF16)
    keep_ref[...] = both_ref[core]
    give_ref[...] = both_ref[1 - core]


def finish_kernel(r_ref, text_ref, text_out, qkv_out, out_out, stack_ref, line_ref):
    total = r_ref[0].astype(F32)
    for s in range(1, 8):
        total = total + r_ref[s].astype(F32)
    unit_grad = total[384:396, :]
    for i in range(12):
        line_ref[i:i + 1, :] = text_ref[:, i * 128:(i + 1) * 128].astype(F32)
    text = line_ref[...]
    inv = lax.rsqrt(jnp.sum(text * text, keepdims=True) + EPS)
    unit = text * inv
    line_ref[...] = (unit_grad - unit * jnp.sum(unit * unit_grad, keepdims=True)) * inv
    for i in range(12):
        text_out[:, i * 128:(i + 1) * 128] = line_ref[i:i + 1, :]
    pad = jnp.zeros((32, 128), F32)
    for c in range(2):
        for i in range(2):
            at = (c * 2 + i) * 96
            turned = jnp.concatenate([total[at:at + 96, :], pad], axis=0).T
            rows = 128 if i == 0 else 64
            qkv_out[c, i * 128:i * 128 + rows, :] = turned[0:rows, 0:96]
    lane = lanes((96, 128))
    group = lax.shift_right_logical(lane, 3) - 8
    factors = []
    for s in range(8):
        for c in range(2):
            block = r_ref[s, (c * 2 + 1) * 96:(c * 2 + 2) * 96, :]
            factors.append(block)
            rolled = pltpu.roll(block.astype(F32), 96, axis=1)
            for g in range(4):
                at = (s * 2 + c) * 128
                stack_ref[g * 96:(g + 1) * 96, at:at + 128] = jnp.where(
                    group == g, rolled, 0.0
                ).astype(BF16)
    product = dot(stack_ref[...], jnp.concatenate(factors, axis=1), LAST)
    qkv_out[2] = product[0:192, :]
    out_out[...] = product[192:384, :]


HERE = pl.BlockSpec(memory_space=pltpu.VMEM)
ANY = pl.BlockSpec(memory_space=pl.ANY)
SMEM = pl.BlockSpec(memory_space=pltpu.SMEM)


def call(kernel, outs, scratch, *args, specs=None, params=PARAMS):
    return pl.pallas_call(
        kernel,
        out_shape=[jax.ShapeDtypeStruct(*o) for o in outs],
        in_specs=specs or [HERE] * len(args),
        out_specs=[HERE] * len(outs),
        scratch_shapes=[pltpu.VMEM(*s) if isinstance(s, tuple) else s for s in scratch],
        compiler_params=params,
    )(*args)


def over_mp(block, dz, dy):
    route = [(i, ((i // 2 + dz) % 4) * 2 + (i % 2 + dy) % 2) for i in range(MP)]
    return lax.ppermute(block, "mp", route)


def body(tokens, norm_gain, qkv_weight, out_weight, text_embed, log_temp, logit_bias):
    own, token_sum = call(
        norm_kernel,
        [((64, D), BF16), ((IMG, D), F32)],
        [((12 * 64, 128), F32)],
        tokens, norm_gain.reshape(12, 128),
    )
    across = over_mp(own, 0, 1)
    far = over_mp(own, 2, 0)
    ahead = over_mp(own, 1, 0)
    behind = over_mp(own, 3, 0)
    own, text_embed = lax.optimization_barrier((own, text_embed))
    lines, = call(line_kernel, [((DP, 16, 128), BF16)], [((16, 128), F32)], text_embed)
    across, lines = lax.optimization_barrier((across, lines))
    texts = lax.all_to_all(lines, "dp", 0, 0)
    shards = [
        own, across, ahead, behind, far,
        over_mp(across, 1, 0), over_mp(across, 3, 0), over_mp(far, 0, 1),
    ]
    part, qkv, probs, attended, scalars = call(
        forward_kernel,
        [
            ((IMG, D), BF16), ((3, 512, WIDTH), BF16), ((16, 64, 64), BF16),
            ((IMG, WIDTH), F32), ((2, 128), F32),
        ],
        [((512, WIDTH), F32)],
        *shards, qkv_weight, out_weight, token_sum, log_temp, logit_bias,
        specs=[HERE] * (MP + 3) + [SMEM] * 2,
        params=pltpu.CompilerParams(vmem_limit_bytes=FULL),
    )
    joined, = call(join_kernel, [((MP, 24, D), BF16)], [((DP * 16, 128), F32)], part, texts)
    parts = lax.all_to_all(joined, "mp", 0, 0)
    keep, give = call(
        backward_kernel,
        [((8, ROWS, 128), BF16)] * 2,
        [
            ((512, 512), F32), ((256, 128), F32), ((256, 128), F32), ((2, 8, ROWS, 128), BF16),
        ],
        *shards, parts, qkv, probs, attended, scalars, out_weight,
    )
    other = lax.ppermute(give, "dp", [(i, i ^ 1) for i in range(DP)])
    send = (keep.astype(F32) + other.astype(F32)).astype(BF16)
    received = lax.all_to_all(
        send, "dp", 0, 0, axis_index_groups=[list(range(c, DP, 2)) for c in range(2)]
    )
    text_grad, qkv_grad, out_grad = call(
        finish_kernel,
        [((1, D), F32), ((3, WIDTH, 96), F32), ((WIDTH, 96), F32)],
        [((384, 2048), BF16), ((12, 128), F32)],
        received, text_embed,
    )
    return (text_grad, qkv_grad, out_grad)


def solution(mesh):
    placed = (
        P("dp", "mp"),
        P(),
        P(None, "mp", None),
        P("mp", None),
        P(("dp", "mp"), None),
        P(),
        P(),
    )
    return jax.shard_map(
        body,
        mesh=mesh,
        in_specs=placed,
        out_specs=(P(("dp", "mp"), None), P(None, "mp", "dp"), P("mp", "dp")),
        check_vma=False,
    )
```

```python
import math

import jax
import jax.numpy as jnp
from jax import lax
from jax.experimental import pallas as pl
from jax.experimental.pallas import tpu as pltpu
from jax.sharding import PartitionSpec as P

D = 1536
DH = 96
TOK = 64
IMG = 8
MP = 8
DP = 16
TEXT = DP * MP
WIDTH = 192
EPS = 1e-06
F32 = jnp.float32
BF16 = jnp.bfloat16
SCALE = 1.0 / math.sqrt(DH)
ROWS = 400
LAST = (((1,), (1,)), ((), ()))
FIRST = (((0,), (0,)), ((), ()))
PARAMS = pltpu.CompilerParams(vmem_limit_bytes=48 * 1024 * 1024)


def dot(a, b, dims):
    return lax.dot_general(a, b, dims, preferred_element_type=F32)


def pieces(a, n):
    out = []
    for _ in range(n):
        p = a.astype(BF16)
        out.append(p)
        a = a - p.astype(F32)
    return out


def lanes(shape):
    return lax.broadcasted_iota(jnp.int32, shape, len(shape) - 1)


def norm_kernel(tok_ref, out_ref, sum_ref, rows_ref):
    total = jnp.zeros((IMG, D), F32)
    for t in range(8):
        x = tok_ref[:, t * D:(t + 1) * D].astype(F32)
        center = x - jnp.mean(x, axis=-1, keepdims=True)
        spread = jnp.mean(center * center, axis=-1, keepdims=True)
        row = center * lax.rsqrt(spread + EPS)
        for i in range(12):
            rows_ref[pl.ds(i * 64 + t, IMG, stride=8), :] = row[:, i * 128:(i + 1) * 128]
        total = total + x
    sum_ref[...] = total
    out_ref[0:64, :] = jnp.concatenate(
        [rows_ref[i * 64:(i + 1) * 64, :] for i in range(12)], axis=1
    ).astype(BF16)
    out_ref[64:72, :] = jnp.zeros((8, D), BF16)


def load_kernel(
    w_hbm, wo_hbm, gain_ref, temp_ref, bias_ref, w_ref, wo_ref, scalar_ref, raw_ref, sems
):
    copies = [
        pltpu.make_async_copy(w_hbm, raw_ref, sems.at[0]),
        pltpu.make_async_copy(wo_hbm, wo_ref, sems.at[1]),
    ]
    for copy in copies:
        copy.start()
    scalar_ref[0:1, :] = jnp.exp(jnp.full((1, 128), temp_ref[0], F32))
    scalar_ref[1:2, :] = jnp.full((1, 128), bias_ref[0], F32)
    copies[0].wait()
    for i in range(12):
        part = slice(i * 128, (i + 1) * 128)
        for c in range(3):
            scaled = raw_ref[c, :, part].astype(F32) * gain_ref[i:i + 1, :]
            w_ref[c, :, part] = scaled.astype(BF16)
    copies[1].wait()


STEPS = ((0, 0), (0, 1), (1, 0), (3, 0), (2, 0), (1, 1), (3, 1), (2, 1))


def source(slot, step):
    dz, dy = STEPS[step]
    return lax.rem(lax.div(slot, 2) + 4 - dz, 4) * 2 + lax.rem(lax.rem(slot, 2) + dy, 2)


def text_kernel(*refs):
    shards, (out_ref, line_ref) = refs[:MP], refs[MP:]
    slot = lax.axis_index("mp")
    core = lax.rem(lax.axis_index("dp"), 2)
    for s in range(MP):
        two = shards[s][64:72, :].astype(F32)
        for i in range(2):
            at = lax.rem(core + i, 2) * 8 + source(slot, s)
            line_ref[pl.ds(at, 1), :] = two[i:i + 1, :]
    out_ref[...] = line_ref[...].astype(BF16)


def forward_kernel(*refs):
    shards, (w_ref, wo_ref, sum_ref), refs = refs[:MP], refs[MP:MP + 3], refs[MP + 3:]
    part_ref, qkv_ref, probs_ref, att_ref, wide_ref = refs
    normed = jnp.concatenate([r[0:64, :] for r in shards], axis=0)
    for c in range(3):
        wide_ref[...] = dot(normed, w_ref[c], LAST)
        for b in range(IMG):
            block = jnp.concatenate(
                [wide_ref[(s * 8 + b) * 8:(s * 8 + b) * 8 + 8, :] for s in range(MP)], axis=0
            )
            qkv_ref[c, b * 64:(b + 1) * 64, :] = block.astype(BF16)
    lane = lanes((64, WIDTH))
    for b in range(IMG):
        rows = slice(b * 64, (b + 1) * 64)
        q, k = qkv_ref[0, rows, :], qkv_ref[1, rows, :]
        v = qkv_ref[2, rows, :].astype(F32)
        columns = []
        for h in range(2):
            inside = lane < DH if h == 0 else lane >= DH
            score = dot(k, jnp.where(inside, q, jnp.zeros_like(q)), LAST) * SCALE
            weights = jnp.exp(score)
            probs = (weights / jnp.sum(weights, axis=0, keepdims=True)).astype(BF16)
            probs_ref[b * 2 + h] = probs
            columns.append(jnp.sum(probs.astype(F32), axis=1, keepdims=True))
        attended = jnp.sum(jnp.where(lane < DH, columns[0], columns[1]) * v, axis=0, keepdims=True)
        att_ref[b:b + 1, :] = attended
    high, low = pieces(att_ref[...], 2)
    branch = dot(jnp.concatenate([high, low], axis=0), wo_ref[...], (((1,), (0,)), ((), ())))
    part = ((branch[0:8] + branch[8:16] + sum_ref[...]) * (1.0 / TOK)).astype(BF16)
    for d in range(MP):
        part_ref[d] = part


def backward_kernel(*refs):
    shards, texts, refs = refs[:MP], refs[MP:MP + 2], refs[MP + 2:]
    part_ref, qkv_ref, probs_ref, att_ref, scalar_ref, wo_ref = refs[:6]
    keep_ref, give_ref, grad_ref, turn_ref, text_ref, both_ref = refs[6:]
    me = lax.axis_index("dp")
    slot = lax.axis_index("mp")
    core = lax.rem(me, 2)
    pooled = jnp.zeros((IMG, D), F32)
    for s in range(MP):
        pooled = pooled + part_ref[s].astype(F32)
    scale = scalar_ref[0:1, :]
    image_inv = lax.rsqrt(jnp.sum(pooled * pooled, axis=-1, keepdims=True) + EPS)
    unit = pooled * image_inv
    text = jnp.concatenate([r[...] for r in texts], axis=0)
    wide_text = text.astype(F32)
    square = pieces(wide_text * wide_text, 2)
    ones = jnp.ones((IMG, D), BF16)
    text_inv = lax.rsqrt(dot(ones, square[0], LAST) + dot(ones, square[1], LAST) + EPS)
    cosine = dot(jnp.concatenate(pieces(unit, 3), axis=0), text, LAST)
    cosine = (cosine[0:8] + cosine[8:16] + cosine[16:24]) * text_inv
    logits = scale * cosine + scalar_ref[1:2, :]
    image_row = lax.broadcasted_iota(jnp.int32, (IMG, TEXT), 0)
    own = lanes((IMG, TEXT)) == core * MP + image_row
    pair = scale * (jax.nn.sigmoid(logits) - jnp.where(own, 1.0, 0.0))
    unit_grad = dot(
        jnp.concatenate(pieces(pair * text_inv, 3), axis=0), text, (((1,), (0,)), ((), ()))
    )
    unit_grad = unit_grad[0:8] + unit_grad[8:16] + unit_grad[16:24]
    pooled_grad = (unit_grad - unit * jnp.sum(unit * unit_grad, axis=-1, keepdims=True)) * image_inv
    resid = (pooled_grad * (1.0 / TOK)).astype(BF16)
    column = lax.broadcasted_iota(jnp.int32, (TEXT, DP), 0)
    owner = lanes((TEXT, DP))
    step_x = lax.rem(lax.rem(lax.div(me, 2), 4) - lax.rem(lax.div(owner, 2), 4) + 4, 4)
    step_y = lax.rem(lax.div(me, 8) + lax.div(owner, 8), 2)
    place = step_y * 64 + step_x * 16 + lax.rem(owner, 2) * MP + slot
    chosen = jnp.where(column == place, 1.0, 0.0).astype(BF16)
    mine = dot(jnp.concatenate(pieces(pair, 3), axis=0), chosen, (((1,), (0,)), ((), ())))
    pair_high, pair_low = pieces(mine[0:8] + mine[8:16] + mine[16:24], 2)
    unit_high, unit_low = pieces(unit, 2)
    text_grad = dot(
        jnp.concatenate([pair_high, pair_high, pair_low], axis=0),
        jnp.concatenate([unit_high, unit_low, unit_high], axis=0),
        FIRST,
    )
    text_ref[...] = jnp.zeros_like(text_ref)
    for i in range(12):
        text_ref[pl.ds(i, DP, stride=16), :] = text_grad[0:DP, i * 128:(i + 1) * 128]
    attend = dot(resid, wo_ref[...], LAST).astype(BF16)
    wide_attend = attend.astype(F32)
    lane = lanes((64, WIDTH))
    slim = lanes((64, 64))
    for b in range(IMG):
        rows = slice(b * 64, (b + 1) * 64)
        q, k = qkv_ref[0, rows, :], qkv_ref[1, rows, :]
        product = qkv_ref[2, rows, :].astype(F32) * wide_attend[b:b + 1, :]
        query_grad, key_grad, factor = [], [], jnp.zeros((64, 64), F32)
        for h in range(2):
            inside = lane < DH if h == 0 else lane >= DH
            prob_grad = jnp.sum(jnp.where(inside, product, 0.0), axis=1, keepdims=True)
            probs = probs_ref[b * 2 + h].astype(F32)
            mean = jnp.sum(probs * prob_grad, axis=0, keepdims=True)
            score_grad = (probs * (prob_grad - mean) * SCALE).astype(BF16)
            query_grad.append(dot(score_grad, k, FIRST))
            key_grad.append(dot(score_grad, q, (((1,), (0,)), ((), ()))))
            column = jnp.sum(probs, axis=1, keepdims=True)
            factor = factor + jnp.where(slim == h * 8 + b, column, 0.0)
        query_grad = jnp.where(lane < DH, query_grad[0], query_grad[1])
        key_grad = jnp.where(lane < DH, key_grad[0], key_grad[1])
        first = jnp.where(core == 0, factor, 0.0)
        full = jnp.concatenate([query_grad, first, key_grad, factor - first], axis=1)
        for s in range(MP):
            grad_ref[(s * 8 + b) * 8:(s * 8 + b) * 8 + 8, :] = full[s * 8:s * 8 + 8, :]
    turn_ref[...] = jnp.zeros_like(turn_ref)
    start = pl.multiple_of(core * 128, 128)
    for h in range(2):
        part = slice(h * DH, (h + 1) * DH)
        turn_ref[pl.ds(start + 96 + h * 8, 8), 0:DH] = wide_attend[:, part]
        turn_ref[pl.ds(start + 112 + h * 8, 8), 0:DH] = att_ref[:, part]
    turned = [turn_ref[i * 128:(i + 1) * 128, :].T[0:DH, :] for i in range(2)]
    place = lanes((IMG, 512)) - lax.broadcasted_iota(jnp.int32, (IMG, 512), 0) - core * 256
    spot = jnp.where((place == 208) | (place == 216), 1.0, 0.0).astype(BF16)
    normed = jnp.concatenate([r[0:64, :] for r in shards], axis=0)
    grads = grad_ref[...].astype(BF16)
    for c in range(4):
        columns = slice(c * 384, (c + 1) * 384)
        y = dot(normed[:, columns], grads, FIRST) + dot(resid[:, columns], spot, FIRST)
        for j in range(4):
            d = c * 4 + j
            for i in range(4):
                block = y[j * 96:(j + 1) * 96, i * 128:(i + 1) * 128]
                if i % 2 == 1:
                    block = block + turned[i // 2]
                both_ref[d % 2, d // 2, i * 96:(i + 1) * 96, :] = block.astype(BF16)
            both_ref[d % 2, d // 2, 384:400, :] = text_ref[d * 16:(d + 1) * 16, :].astype(BF16)
    keep_ref[...] = both_ref[core]
    give_ref[...] = both_ref[1 - core]


def finish_kernel(r_ref, text_ref, gain_ref, text_out, qkv_out, out_out, stack_ref, line_ref):
    total = r_ref[0].astype(F32)
    for s in range(1, 8):
        total = total + r_ref[s].astype(F32)
    unit_grad = total[384:396, :]
    for i in range(12):
        line_ref[i:i + 1, :] = text_ref[:, i * 128:(i + 1) * 128].astype(F32)
    text = line_ref[...]
    inv = lax.rsqrt(jnp.sum(text * text, keepdims=True) + EPS)
    unit = text * inv
    line_ref[...] = (unit_grad - unit * jnp.sum(unit * unit_grad, keepdims=True)) * inv
    for i in range(12):
        text_out[:, i * 128:(i + 1) * 128] = line_ref[i:i + 1, :]
    first = lax.axis_index("dp") * 96
    shift = lax.rem(first, 128)
    above = gain_ref[pl.ds(lax.div(first, 128), 1), :]
    below = gain_ref[pl.ds(jnp.minimum(lax.div(first, 128) + 1, 11), 1), :]
    gain = jnp.where(lanes((1, 128)) < shift, below, above)
    gain = pltpu.roll(gain, lax.rem(128 - shift, 128), axis=1)[:, 0:96]
    pad = jnp.zeros((32, 128), F32)
    for c in range(2):
        for i in range(2):
            at = (c * 2 + i) * 96
            turned = jnp.concatenate([total[at:at + 96, :], pad], axis=0).T
            rows = 128 if i == 0 else 64
            qkv_out[c, i * 128:i * 128 + rows, :] = turned[0:rows, 0:96] * gain
    lane = lanes((96, 128))
    group = lax.shift_right_logical(lane, 3) - 8
    factors = []
    for s in range(8):
        for c in range(2):
            block = r_ref[s, (c * 2 + 1) * 96:(c * 2 + 2) * 96, :]
            factors.append(block)
            rolled = pltpu.roll(block.astype(F32), 96, axis=1).astype(BF16)
            for g in range(4):
                at = (s * 2 + c) * 128
                stack_ref[g * 96:(g + 1) * 96, at:at + 128] = jnp.where(
                    group == g, rolled, jnp.zeros_like(rolled)
                )
    product = dot(stack_ref[...], jnp.concatenate(factors, axis=1), LAST)
    qkv_out[2] = product[0:192, :] * gain
    out_out[...] = product[192:384, :]


HERE = pl.BlockSpec(memory_space=pltpu.VMEM)
ANY = pl.BlockSpec(memory_space=pl.ANY)
SMEM = pl.BlockSpec(memory_space=pltpu.SMEM)


def call(kernel, outs, scratch, *args, specs=None, params=PARAMS):
    return pl.pallas_call(
        kernel,
        out_shape=[jax.ShapeDtypeStruct(*o) for o in outs],
        in_specs=specs or [HERE] * len(args),
        out_specs=[HERE] * len(outs),
        scratch_shapes=[pltpu.VMEM(*s) if isinstance(s, tuple) else s for s in scratch],
        compiler_params=params,
    )(*args)


def over_mp(block, dz, dy):
    route = [(i, ((i // 2 + dz) % 4) * 2 + (i % 2 + dy) % 2) for i in range(MP)]
    return lax.ppermute(block, "mp", route)


def over_dp(block, dy, dx, dc):
    route = [
        (i, ((i // 8 + dy) % 2 * 4 + (i // 2 + dx) % 4) * 2 + (i + dc) % 2) for i in range(DP)
    ]
    return lax.ppermute(block, "dp", route)


def first_step(block):
    far = over_mp(block, 2, 0)
    across, ahead, behind = [over_mp(block, dz, dy) for dz, dy in STEPS[1:4]]
    return [block, across, ahead, behind, far]


def second_step(blocks):
    across, far = blocks[1], blocks[4]
    return [over_mp(across, 1, 0), over_mp(across, 3, 0), over_mp(far, 0, 1)]


def body(tokens, norm_gain, qkv_weight, out_weight, text_embed, log_temp, logit_bias):
    own, token_sum = call(
        norm_kernel,
        [((72, D), BF16), ((IMG, D), F32)],
        [((12 * 64, 128), F32)],
        tokens,
    )
    own = lax.dynamic_update_slice(own, text_embed, (64, 0))
    own = lax.dynamic_update_slice(own, over_dp(text_embed, 0, 0, 1), (65, 0))
    shards = first_step(own)
    shards[1], qkv_weight, out_weight, gain = lax.optimization_barrier(
        (shards[1], qkv_weight, out_weight, norm_gain)
    )
    shards += second_step(shards)
    qkv_weight, out_weight, scalars = call(
        load_kernel,
        [((3, WIDTH, D), BF16), ((WIDTH, D), BF16), ((2, 128), F32)],
        [((3, WIDTH, D), BF16), pltpu.SemaphoreType.DMA((2,))],
        qkv_weight, out_weight, gain.reshape(12, 128), log_temp, logit_bias,
        specs=[ANY, ANY, HERE, SMEM, SMEM],
    )
    shards[0], qkv_weight, out_weight = lax.optimization_barrier(
        (shards[0], qkv_weight, out_weight)
    )
    texts, = call(text_kernel, [((16, D), BF16)], [((16, D), F32)], *shards)
    texts = [texts] + [over_dp(texts, 0, dx, 0) for dx in (1, 2, 3)]
    part, qkv, probs, attended = call(
        forward_kernel,
        [
            ((MP, IMG, D), BF16), ((3, 512, WIDTH), BF16),
            ((16, 64, 64), BF16), ((IMG, WIDTH), F32),
        ],
        [((512, WIDTH), F32)],
        *shards, qkv_weight, out_weight, token_sum,
    )
    part, *texts = lax.optimization_barrier((part, *texts))
    texts = jnp.concatenate(texts, axis=0)
    texts = [texts, over_dp(texts, 1, 0, 0)]
    parts = lax.all_to_all(part, "mp", 0, 0)
    keep, give = call(
        backward_kernel,
        [((8, ROWS, 128), BF16)] * 2,
        [((512, 512), F32), ((256, 128), F32), ((256, 128), F32), ((2, 8, ROWS, 128), BF16)],
        *shards, *texts, parts, qkv, probs, attended, scalars, out_weight,
    )
    other = lax.ppermute(give, "dp", [(i, i ^ 1) for i in range(DP)])
    send = (keep.astype(F32) + other.astype(F32)).astype(BF16)
    received = lax.all_to_all(
        send, "dp", 0, 0, axis_index_groups=[list(range(c, DP, 2)) for c in range(2)]
    )
    text_grad, qkv_grad, out_grad = call(
        finish_kernel,
        [((1, D), F32), ((3, WIDTH, 96), F32), ((WIDTH, 96), F32)],
        [((384, 2048), BF16), ((12, 128), F32)],
        received, text_embed, norm_gain.reshape(12, 128),
    )
    return (text_grad, qkv_grad, out_grad)


def solution(mesh):
    placed = (
        P("dp", "mp"),
        P(),
        P(None, "mp", None),
        P("mp", None),
        P(("dp", "mp"), None),
        P(),
        P(),
    )
    return jax.shard_map(
        body,
        mesh=mesh,
        in_specs=placed,
        out_specs=(P(("dp", "mp"), None), P(None, "mp", "dp"), P("mp", "dp")),
        check_vma=False,
    )
```

```python
import math

import jax
import jax.numpy as jnp
from jax import lax
from jax.experimental import pallas as pl
from jax.experimental.pallas import tpu as pltpu
from jax.sharding import PartitionSpec as P

D = 1536
DH = 96
TOK = 64
IMG = 8
MP = 8
DP = 16
TEXT = DP * MP
WIDTH = 192
EPS = 1e-06
F32 = jnp.float32
BF16 = jnp.bfloat16
SCALE = 1.0 / math.sqrt(DH)
ROWS = 400
LAST = (((1,), (1,)), ((), ()))
FIRST = (((0,), (0,)), ((), ()))
PARAMS = pltpu.CompilerParams(vmem_limit_bytes=48 * 1024 * 1024)


def dot(a, b, dims):
    return lax.dot_general(a, b, dims, preferred_element_type=F32)


def pieces(a, n):
    out = []
    for _ in range(n):
        p = a.astype(BF16)
        out.append(p)
        a = a - p.astype(F32)
    return out


def lanes(shape):
    return lax.broadcasted_iota(jnp.int32, shape, len(shape) - 1)


def norm_kernel(tok_ref, out_ref, sum_ref, rows_ref):
    total = jnp.zeros((IMG, D), F32)
    for t in range(8):
        x = tok_ref[:, t * D:(t + 1) * D].astype(F32)
        center = x - jnp.mean(x, axis=-1, keepdims=True)
        spread = jnp.mean(center * center, axis=-1, keepdims=True)
        row = center * lax.rsqrt(spread + EPS)
        for i in range(12):
            rows_ref[pl.ds(i * 64 + t, IMG, stride=8), :] = row[:, i * 128:(i + 1) * 128]
        total = total + x
    sum_ref[...] = total
    out_ref[0:64, :] = jnp.concatenate(
        [rows_ref[i * 64:(i + 1) * 64, :] for i in range(12)], axis=1
    ).astype(BF16)
    out_ref[64:72, :] = jnp.zeros((8, D), BF16)


def scalar_kernel(temp_ref, bias_ref, scalar_ref):
    scalar_ref[0:1, :] = jnp.exp(jnp.full((1, 128), temp_ref[0], F32))
    scalar_ref[1:2, :] = jnp.full((1, 128), bias_ref[0], F32)


def load_kernel(w_hbm, wo_hbm, gain_ref, w_ref, wo_ref, raw_ref, sems):
    copies = [
        pltpu.make_async_copy(w_hbm, raw_ref, sems.at[0]),
        pltpu.make_async_copy(wo_hbm, wo_ref, sems.at[1]),
    ]
    for copy in copies:
        copy.start()
    copies[0].wait()
    for i in range(12):
        part = slice(i * 128, (i + 1) * 128)
        for c in range(3):
            scaled = raw_ref[c, :, part].astype(F32) * gain_ref[i:i + 1, :]
            w_ref[c, :, part] = scaled.astype(BF16)
    copies[1].wait()


STEPS = ((0, 0), (0, 1), (1, 0), (3, 0), (2, 0), (1, 1), (3, 1), (2, 1))


def source(slot, step):
    dz, dy = STEPS[step]
    return lax.rem(lax.div(slot, 2) + 4 - dz, 4) * 2 + lax.rem(lax.rem(slot, 2) + dy, 2)


def text_kernel(*refs):
    shards, (out_ref, line_ref) = refs[:MP], refs[MP:]
    slot = lax.axis_index("mp")
    core = lax.rem(lax.axis_index("dp"), 2)
    for s in range(MP):
        two = shards[s][64:72, :].astype(F32)
        for i in range(2):
            at = lax.rem(core + i, 2) * 8 + source(slot, s)
            line_ref[pl.ds(at, 1), :] = two[i:i + 1, :]
    out_ref[...] = line_ref[...].astype(BF16)


def early_kernel(*refs):
    shards, (w_ref, qkv_ref, wide_ref) = refs[:5], refs[5:]
    normed = jnp.concatenate([r[0:64, :] for r in shards], axis=0)
    for c in range(3):
        wide_ref[...] = dot(normed, w_ref[c], LAST)
        for b in range(IMG):
            block = jnp.concatenate(
                [wide_ref[(s * 8 + b) * 8:(s * 8 + b) * 8 + 8, :] for s in range(5)], axis=0
            )
            qkv_ref[c, b * 40:(b + 1) * 40, :] = block.astype(BF16)


def forward_kernel(*refs):
    shards, (early_ref, w_ref, wo_ref, sum_ref), refs = refs[:3], refs[3:7], refs[7:]
    part_ref, qkv_ref, probs_ref, att_ref, wide_ref = refs
    normed = jnp.concatenate([r[0:64, :] for r in shards], axis=0)
    for c in range(3):
        wide_ref[...] = dot(normed, w_ref[c], LAST)
        for b in range(IMG):
            block = jnp.concatenate(
                [early_ref[c, b * 40:(b + 1) * 40, :].astype(F32)]
                + [wide_ref[(s * 8 + b) * 8:(s * 8 + b) * 8 + 8, :] for s in range(3)], axis=0
            )
            qkv_ref[c, b * 64:(b + 1) * 64, :] = block.astype(BF16)
    lane = lanes((64, WIDTH))
    for b in range(IMG):
        rows = slice(b * 64, (b + 1) * 64)
        q, k = qkv_ref[0, rows, :], qkv_ref[1, rows, :]
        v = qkv_ref[2, rows, :].astype(F32)
        columns = []
        for h in range(2):
            inside = lane < DH if h == 0 else lane >= DH
            score = dot(k, jnp.where(inside, q, jnp.zeros_like(q)), LAST) * SCALE
            weights = jnp.exp(score)
            probs = (weights / jnp.sum(weights, axis=0, keepdims=True)).astype(BF16)
            probs_ref[b * 2 + h] = probs
            columns.append(jnp.sum(probs.astype(F32), axis=1, keepdims=True))
        attended = jnp.sum(jnp.where(lane < DH, columns[0], columns[1]) * v, axis=0, keepdims=True)
        att_ref[b:b + 1, :] = attended
    high, low = pieces(att_ref[...], 2)
    branch = dot(jnp.concatenate([high, low], axis=0), wo_ref[...], (((1,), (0,)), ((), ())))
    part = ((branch[0:8] + branch[8:16] + sum_ref[...]) * (1.0 / TOK)).astype(BF16)
    for d in range(MP):
        part_ref[d] = part


def backward_kernel(*refs):
    shards, texts, refs = refs[:MP], refs[MP:MP + 4], refs[MP + 4:]
    part_ref, qkv_ref, probs_ref, att_ref, scalar_ref, wo_ref = refs[:6]
    keep_ref, give_ref, grad_ref, turn_ref, text_ref, both_ref = refs[6:]
    me = lax.axis_index("dp")
    slot = lax.axis_index("mp")
    core = lax.rem(me, 2)
    pooled = jnp.zeros((IMG, D), F32)
    for s in range(MP):
        pooled = pooled + part_ref[s].astype(F32)
    scale = scalar_ref[0:1, :]
    image_inv = lax.rsqrt(jnp.sum(pooled * pooled, axis=-1, keepdims=True) + EPS)
    unit = pooled * image_inv
    text = jnp.concatenate([r[0:32, :] for r in texts], axis=0)
    wide_text = text.astype(F32)
    square = pieces(wide_text * wide_text, 2)
    ones = jnp.ones((IMG, D), BF16)
    text_inv = lax.rsqrt(dot(ones, square[0], LAST) + dot(ones, square[1], LAST) + EPS)
    cosine = dot(jnp.concatenate(pieces(unit, 3), axis=0), text, LAST)
    cosine = (cosine[0:8] + cosine[8:16] + cosine[16:24]) * text_inv
    logits = scale * cosine + scalar_ref[1:2, :]
    image_row = lax.broadcasted_iota(jnp.int32, (IMG, TEXT), 0)
    own = lanes((IMG, TEXT)) == core * MP + image_row
    pair = scale * (jax.nn.sigmoid(logits) - jnp.where(own, 1.0, 0.0))
    unit_grad = dot(
        jnp.concatenate(pieces(pair * text_inv, 3), axis=0), text, (((1,), (0,)), ((), ()))
    )
    unit_grad = unit_grad[0:8] + unit_grad[8:16] + unit_grad[16:24]
    pooled_grad = (unit_grad - unit * jnp.sum(unit * unit_grad, axis=-1, keepdims=True)) * image_inv
    resid = (pooled_grad * (1.0 / TOK)).astype(BF16)
    column = lax.broadcasted_iota(jnp.int32, (TEXT, DP), 0)
    owner = lanes((TEXT, DP))
    step_x = lax.rem(lax.rem(lax.div(me, 2), 4) - lax.rem(lax.div(owner, 2), 4) + 4, 4)
    step_y = lax.rem(lax.div(me, 8) + lax.div(owner, 8), 2)
    place = step_x * 32 + step_y * 16 + lax.rem(owner, 2) * MP + slot
    chosen = jnp.where(column == place, 1.0, 0.0).astype(BF16)
    mine = dot(jnp.concatenate(pieces(pair, 3), axis=0), chosen, (((1,), (0,)), ((), ())))
    pair_high, pair_low = pieces(mine[0:8] + mine[8:16] + mine[16:24], 2)
    unit_high, unit_low = pieces(unit, 2)
    text_grad = dot(
        jnp.concatenate([pair_high, pair_high, pair_low], axis=0),
        jnp.concatenate([unit_high, unit_low, unit_high], axis=0),
        FIRST,
    )
    text_ref[...] = jnp.zeros_like(text_ref)
    for i in range(12):
        text_ref[pl.ds(i, DP, stride=16), :] = text_grad[0:DP, i * 128:(i + 1) * 128]
    attend = dot(resid, wo_ref[...], LAST).astype(BF16)
    wide_attend = attend.astype(F32)
    lane = lanes((64, WIDTH))
    slim = lanes((64, 64))
    for b in range(IMG):
        rows = slice(b * 64, (b + 1) * 64)
        q, k = qkv_ref[0, rows, :], qkv_ref[1, rows, :]
        product = qkv_ref[2, rows, :].astype(F32) * wide_attend[b:b + 1, :]
        query_grad, key_grad, factor = [], [], jnp.zeros((64, 64), F32)
        for h in range(2):
            inside = lane < DH if h == 0 else lane >= DH
            prob_grad = jnp.sum(jnp.where(inside, product, 0.0), axis=1, keepdims=True)
            probs = probs_ref[b * 2 + h].astype(F32)
            mean = jnp.sum(probs * prob_grad, axis=0, keepdims=True)
            score_grad = (probs * (prob_grad - mean) * SCALE).astype(BF16)
            query_grad.append(dot(score_grad, k, FIRST))
            key_grad.append(dot(score_grad, q, (((1,), (0,)), ((), ()))))
            column = jnp.sum(probs, axis=1, keepdims=True)
            factor = factor + jnp.where(slim == h * 8 + b, column, 0.0)
        query_grad = jnp.where(lane < DH, query_grad[0], query_grad[1])
        key_grad = jnp.where(lane < DH, key_grad[0], key_grad[1])
        first = jnp.where(core == 0, factor, 0.0)
        full = jnp.concatenate([query_grad, first, key_grad, factor - first], axis=1)
        for s in range(MP):
            grad_ref[(s * 8 + b) * 8:(s * 8 + b) * 8 + 8, :] = full[s * 8:s * 8 + 8, :]
    turn_ref[...] = jnp.zeros_like(turn_ref)
    start = pl.multiple_of(core * 128, 128)
    for h in range(2):
        part = slice(h * DH, (h + 1) * DH)
        turn_ref[pl.ds(start + 96 + h * 8, 8), 0:DH] = wide_attend[:, part]
        turn_ref[pl.ds(start + 112 + h * 8, 8), 0:DH] = att_ref[:, part]
    turned = [turn_ref[i * 128:(i + 1) * 128, :].T[0:DH, :] for i in range(2)]
    place = lanes((IMG, 512)) - lax.broadcasted_iota(jnp.int32, (IMG, 512), 0) - core * 256
    spot = jnp.where((place == 208) | (place == 216), 1.0, 0.0).astype(BF16)
    normed = jnp.concatenate([r[0:64, :] for r in shards], axis=0)
    grads = grad_ref[...].astype(BF16)
    for c in range(4):
        columns = slice(c * 384, (c + 1) * 384)
        y = dot(normed[:, columns], grads, FIRST) + dot(resid[:, columns], spot, FIRST)
        for j in range(4):
            d = c * 4 + j
            for i in range(4):
                block = y[j * 96:(j + 1) * 96, i * 128:(i + 1) * 128]
                if i % 2 == 1:
                    block = block + turned[i // 2]
                both_ref[d % 2, d // 2, i * 96:(i + 1) * 96, :] = block.astype(BF16)
            both_ref[d % 2, d // 2, 384:400, :] = text_ref[d * 16:(d + 1) * 16, :].astype(BF16)
    keep_ref[...] = both_ref[core]
    give_ref[...] = both_ref[1 - core]


def finish_kernel(r_ref, text_ref, gain_ref, text_out, qkv_out, out_out, stack_ref, line_ref):
    total = r_ref[0].astype(F32)
    for s in range(1, 8):
        total = total + r_ref[s].astype(F32)
    unit_grad = total[384:396, :]
    for i in range(12):
        line_ref[i:i + 1, :] = text_ref[:, i * 128:(i + 1) * 128].astype(F32)
    text = line_ref[...]
    inv = lax.rsqrt(jnp.sum(text * text, keepdims=True) + EPS)
    unit = text * inv
    line_ref[...] = (unit_grad - unit * jnp.sum(unit * unit_grad, keepdims=True)) * inv
    for i in range(12):
        text_out[:, i * 128:(i + 1) * 128] = line_ref[i:i + 1, :]
    first = lax.axis_index("dp") * 96
    shift = lax.rem(first, 128)
    above = gain_ref[pl.ds(lax.div(first, 128), 1), :]
    below = gain_ref[pl.ds(jnp.minimum(lax.div(first, 128) + 1, 11), 1), :]
    gain = jnp.where(lanes((1, 128)) < shift, below, above)
    gain = pltpu.roll(gain, lax.rem(128 - shift, 128), axis=1)[:, 0:96]
    pad = jnp.zeros((32, 128), F32)
    for c in range(2):
        for i in range(2):
            at = (c * 2 + i) * 96
            turned = jnp.concatenate([total[at:at + 96, :], pad], axis=0).T
            rows = 128 if i == 0 else 64
            qkv_out[c, i * 128:i * 128 + rows, :] = turned[0:rows, 0:96] * gain
    lane = lanes((96, 128))
    group = lax.shift_right_logical(lane, 3) - 8
    factors = []
    for s in range(8):
        for c in range(2):
            block = r_ref[s, (c * 2 + 1) * 96:(c * 2 + 2) * 96, :]
            factors.append(block)
            rolled = pltpu.roll(block.astype(F32), 96, axis=1).astype(BF16)
            for g in range(4):
                at = (s * 2 + c) * 128
                stack_ref[g * 96:(g + 1) * 96, at:at + 128] = jnp.where(
                    group == g, rolled, jnp.zeros_like(rolled)
                )
    product = dot(stack_ref[...], jnp.concatenate(factors, axis=1), LAST)
    qkv_out[2] = product[0:192, :] * gain
    out_out[...] = product[192:384, :]


HERE = pl.BlockSpec(memory_space=pltpu.VMEM)
ANY = pl.BlockSpec(memory_space=pl.ANY)
SMEM = pl.BlockSpec(memory_space=pltpu.SMEM)


def call(kernel, outs, scratch, *args, specs=None, params=PARAMS):
    return pl.pallas_call(
        kernel,
        out_shape=[jax.ShapeDtypeStruct(*o) for o in outs],
        in_specs=specs or [HERE] * len(args),
        out_specs=[HERE] * len(outs),
        scratch_shapes=[pltpu.VMEM(*s) if isinstance(s, tuple) else s for s in scratch],
        compiler_params=params,
    )(*args)


def over_mp(block, dz, dy):
    route = [(i, ((i // 2 + dz) % 4) * 2 + (i % 2 + dy) % 2) for i in range(MP)]
    return lax.ppermute(block, "mp", route)


def over_dp(block, dy, dx, dc):
    route = [
        (i, ((i // 8 + dy) % 2 * 4 + (i // 2 + dx) % 4) * 2 + (i + dc) % 2) for i in range(DP)
    ]
    return lax.ppermute(block, "dp", route)


def first_step(block):
    far = over_mp(block, 2, 0)
    across, ahead, behind = [over_mp(block, dz, dy) for dz, dy in STEPS[1:4]]
    return [block, across, ahead, behind, far]


def second_step(blocks):
    across, far = blocks[1], blocks[4]
    return [over_mp(across, 1, 0), over_mp(across, 3, 0), over_mp(far, 0, 1)]


def body(tokens, norm_gain, qkv_weight, out_weight, text_embed, log_temp, logit_bias):
    own, token_sum = call(
        norm_kernel,
        [((72, D), BF16), ((IMG, D), F32)],
        [((12 * 64, 128), F32)],
        tokens,
    )
    own = lax.dynamic_update_slice(own, text_embed, (64, 0))
    own = lax.dynamic_update_slice(own, over_dp(text_embed, 0, 0, 1), (65, 0))
    shards = first_step(own)
    own, qkv_weight, out_weight, gain = lax.optimization_barrier(
        (own, qkv_weight, out_weight, norm_gain)
    )
    qkv_weight, out_weight = call(
        load_kernel,
        [((3, WIDTH, D), BF16), ((WIDTH, D), BF16)],
        [((3, WIDTH, D), BF16), pltpu.SemaphoreType.DMA((2,))],
        qkv_weight, out_weight, gain.reshape(12, 128), specs=[ANY, ANY, HERE],
    )
    shards[1], qkv_weight, out_weight = lax.optimization_barrier(
        (shards[1], qkv_weight, out_weight)
    )
    shards += second_step(shards)
    shards[2], log_temp, logit_bias = lax.optimization_barrier((shards[2], log_temp, logit_bias))
    scalars, = call(scalar_kernel, [((2, 128), F32)], [], log_temp, logit_bias, specs=[SMEM] * 2)
    shards[0], scalars = lax.optimization_barrier((shards[0], scalars))
    early, = call(
        early_kernel, [((3, 320, WIDTH), BF16)], [((320, WIDTH), F32)], *shards[:5], qkv_weight
    )
    shards[0], early = lax.optimization_barrier((shards[0], early))
    texts, = call(text_kernel, [((16, D), BF16)], [((16, D), F32)], *shards)
    texts = [texts, over_dp(texts, 1, 0, 0)]
    part, qkv, probs, attended = call(
        forward_kernel,
        [
            ((MP, IMG, D), BF16), ((3, 512, WIDTH), BF16),
            ((16, 64, 64), BF16), ((IMG, WIDTH), F32),
        ],
        [((192, WIDTH), F32)],
        *shards[5:], early, qkv_weight, out_weight, token_sum,
    )
    part, *texts = lax.optimization_barrier((part, *texts))
    texts = jnp.concatenate(texts + texts, axis=0)
    texts = [texts] + [over_dp(texts, 0, dx, 0) for dx in (1, 2, 3)]
    parts = lax.all_to_all(part, "mp", 0, 0)
    keep, give = call(
        backward_kernel,
        [((8, ROWS, 128), BF16)] * 2,
        [((512, 512), F32), ((256, 128), F32), ((256, 128), F32), ((2, 8, ROWS, 128), BF16)],
        *shards, *texts, parts, qkv, probs, attended, scalars, out_weight,
    )
    other = lax.ppermute(give, "dp", [(i, i ^ 1) for i in range(DP)])
    send = (keep.astype(F32) + other.astype(F32)).astype(BF16)
    received = lax.all_to_all(
        send, "dp", 0, 0, axis_index_groups=[list(range(c, DP, 2)) for c in range(2)]
    )
    text_grad, qkv_grad, out_grad = call(
        finish_kernel,
        [((1, D), F32), ((3, WIDTH, 96), F32), ((WIDTH, 96), F32)],
        [((384, 2048), BF16), ((12, 128), F32)],
        received, text_embed, norm_gain.reshape(12, 128),
    )
    return (text_grad, qkv_grad, out_grad)


def solution(mesh):
    placed = (
        P("dp", "mp"),
        P(),
        P(None, "mp", None),
        P("mp", None),
        P(("dp", "mp"), None),
        P(),
        P(),
    )
    return jax.shard_map(
        body,
        mesh=mesh,
        in_specs=placed,
        out_specs=(P(("dp", "mp"), None), P(None, "mp", "dp"), P("mp", "dp")),
        check_vma=False,
    )
```

```python
import functools
import math

import jax
import jax.numpy as jnp
from jax import lax
from jax.experimental import pallas as pl
from jax.experimental.pallas import tpu as pltpu
from jax.sharding import PartitionSpec as P

D = 1536
DH = 96
TOK = 64
IMG = 8
MP = 8
DP = 16
TEXT = DP * MP
WIDTH = 192
EPS = 1e-06
F32 = jnp.float32
BF16 = jnp.bfloat16
SCALE = 1.0 / math.sqrt(DH)
ROWS = 400
LAST = (((1,), (1,)), ((), ()))
FIRST = (((0,), (0,)), ((), ()))
PARAMS = pltpu.CompilerParams(vmem_limit_bytes=48 * 1024 * 1024)


def dot(a, b, dims):
    return lax.dot_general(a, b, dims, preferred_element_type=F32)


def pieces(a, n):
    out = []
    for _ in range(n):
        p = a.astype(BF16)
        out.append(p)
        a = a - p.astype(F32)
    return out


def lanes(shape):
    return lax.broadcasted_iota(jnp.int32, shape, len(shape) - 1)


def norm_kernel(tok_ref, out_ref, sum_ref, rows_ref):
    total = jnp.zeros((IMG, D), F32)
    for t in range(8):
        x = tok_ref[:, t * D:(t + 1) * D].astype(F32)
        center = x - jnp.mean(x, axis=-1, keepdims=True)
        spread = jnp.mean(center * center, axis=-1, keepdims=True)
        row = center * lax.rsqrt(spread + EPS)
        for i in range(12):
            rows_ref[pl.ds(i * 64 + t, IMG, stride=8), :] = row[:, i * 128:(i + 1) * 128]
        total = total + x
    sum_ref[...] = total
    out_ref[0:64, :] = jnp.concatenate(
        [rows_ref[i * 64:(i + 1) * 64, :] for i in range(12)], axis=1
    ).astype(BF16)
    out_ref[64:72, :] = jnp.zeros((8, D), BF16)


def scalar_kernel(temp_ref, bias_ref, scalar_ref):
    scalar_ref[0:1, :] = jnp.exp(jnp.full((1, 128), temp_ref[0], F32))
    scalar_ref[1:2, :] = jnp.full((1, 128), bias_ref[0], F32)


def load_kernel(w_hbm, wo_hbm, gain_ref, w_ref, wo_ref, raw_ref, sems):
    copies = [
        pltpu.make_async_copy(w_hbm, raw_ref, sems.at[0]),
        pltpu.make_async_copy(wo_hbm, wo_ref, sems.at[1]),
    ]
    for copy in copies:
        copy.start()
    copies[0].wait()
    for i in range(12):
        part = slice(i * 128, (i + 1) * 128)
        for c in range(3):
            scaled = raw_ref[c, :, part].astype(F32) * gain_ref[i:i + 1, :]
            w_ref[c, :, part] = scaled.astype(BF16)
    copies[1].wait()


STEPS = ((0, 0), (0, 1), (1, 0), (3, 0), (2, 0), (1, 1), (3, 1), (2, 1))


def source(slot, step):
    dz, dy = STEPS[step]
    return lax.rem(lax.div(slot, 2) + 4 - dz, 4) * 2 + lax.rem(lax.rem(slot, 2) + dy, 2)


def text_kernel(first, count, *refs):
    shards, (kept_ref, out_ref) = refs[:count], refs[count:]
    slot = lax.axis_index("mp")
    core = lax.rem(lax.axis_index("dp"), 2)
    row = lax.broadcasted_iota(jnp.int32, (16, D), 0)
    total = kept_ref[...]
    for s in range(count):
        two = shards[s][64:72, :].astype(F32)
        for i in range(2):
            at = lax.rem(core + i, 2) * 8 + source(slot, first + s)
            total = jnp.where(row == at, two[i:i + 1, :], total)
    out_ref[...] = total.astype(out_ref.dtype)


def early_kernel(*refs):
    shards, (w_ref, qkv_ref, wide_ref) = refs[:5], refs[5:]
    normed = jnp.concatenate([r[0:64, :] for r in shards], axis=0)
    for c in range(3):
        wide_ref[...] = dot(normed, w_ref[c], LAST)
        for b in range(IMG):
            block = jnp.concatenate(
                [wide_ref[(s * 8 + b) * 8:(s * 8 + b) * 8 + 8, :] for s in range(5)], axis=0
            )
            qkv_ref[c, b * 40:(b + 1) * 40, :] = block.astype(BF16)


def forward_kernel(*refs):
    shards, (early_ref, w_ref, wo_ref, sum_ref), refs = refs[:3], refs[3:7], refs[7:]
    part_ref, qkv_ref, probs_ref, att_ref, wide_ref = refs
    normed = jnp.concatenate([r[0:64, :] for r in shards], axis=0)
    for c in range(3):
        wide_ref[...] = dot(normed, w_ref[c], LAST)
        for b in range(IMG):
            block = jnp.concatenate(
                [early_ref[c, b * 40:(b + 1) * 40, :].astype(F32)]
                + [wide_ref[(s * 8 + b) * 8:(s * 8 + b) * 8 + 8, :] for s in range(3)], axis=0
            )
            qkv_ref[c, b * 64:(b + 1) * 64, :] = block.astype(BF16)
    lane = lanes((64, WIDTH))
    for b in range(IMG):
        rows = slice(b * 64, (b + 1) * 64)
        q, k = qkv_ref[0, rows, :], qkv_ref[1, rows, :]
        v = qkv_ref[2, rows, :].astype(F32)
        columns = []
        for h in range(2):
            inside = lane < DH if h == 0 else lane >= DH
            score = dot(k, jnp.where(inside, q, jnp.zeros_like(q)), LAST) * SCALE
            weights = jnp.exp(score)
            probs = (weights / jnp.sum(weights, axis=0, keepdims=True)).astype(BF16)
            probs_ref[b * 2 + h] = probs
            columns.append(jnp.sum(probs.astype(F32), axis=1, keepdims=True))
        attended = jnp.sum(jnp.where(lane < DH, columns[0], columns[1]) * v, axis=0, keepdims=True)
        att_ref[b:b + 1, :] = attended
    high, low = pieces(att_ref[...], 2)
    branch = dot(jnp.concatenate([high, low], axis=0), wo_ref[...], (((1,), (0,)), ((), ())))
    part = ((branch[0:8] + branch[8:16] + sum_ref[...]) * (1.0 / TOK)).astype(BF16)
    for d in range(MP):
        part_ref[d] = part


def backward_kernel(*refs):
    shards, texts, refs = refs[:MP], refs[MP:MP + 4], refs[MP + 4:]
    part_ref, qkv_ref, probs_ref, att_ref, scalar_ref, wo_ref = refs[:6]
    keep_ref, give_ref, grad_ref, turn_ref, text_ref, both_ref = refs[6:]
    me = lax.axis_index("dp")
    slot = lax.axis_index("mp")
    core = lax.rem(me, 2)
    pooled = jnp.zeros((IMG, D), F32)
    for s in range(MP):
        pooled = pooled + part_ref[s].astype(F32)
    scale = scalar_ref[0:1, :]
    image_inv = lax.rsqrt(jnp.sum(pooled * pooled, axis=-1, keepdims=True) + EPS)
    unit = pooled * image_inv
    text = jnp.concatenate([r[0:32, :] for r in texts], axis=0)
    wide_text = text.astype(F32)
    square = pieces(wide_text * wide_text, 2)
    ones = jnp.ones((IMG, D), BF16)
    text_inv = lax.rsqrt(dot(ones, square[0], LAST) + dot(ones, square[1], LAST) + EPS)
    cosine = dot(jnp.concatenate(pieces(unit, 3), axis=0), text, LAST)
    cosine = (cosine[0:8] + cosine[8:16] + cosine[16:24]) * text_inv
    logits = scale * cosine + scalar_ref[1:2, :]
    image_row = lax.broadcasted_iota(jnp.int32, (IMG, TEXT), 0)
    own = lanes((IMG, TEXT)) == core * MP + image_row
    pair = scale * (jax.nn.sigmoid(logits) - jnp.where(own, 1.0, 0.0))
    unit_grad = dot(
        jnp.concatenate(pieces(pair * text_inv, 3), axis=0), text, (((1,), (0,)), ((), ()))
    )
    unit_grad = unit_grad[0:8] + unit_grad[8:16] + unit_grad[16:24]
    pooled_grad = (unit_grad - unit * jnp.sum(unit * unit_grad, axis=-1, keepdims=True)) * image_inv
    resid = (pooled_grad * (1.0 / TOK)).astype(BF16)
    column = lax.broadcasted_iota(jnp.int32, (TEXT, DP), 0)
    owner = lanes((TEXT, DP))
    step_x = lax.rem(lax.rem(lax.div(me, 2), 4) - lax.rem(lax.div(owner, 2), 4) + 4, 4)
    step_y = lax.rem(lax.div(me, 8) + lax.div(owner, 8), 2)
    place = step_x * 32 + step_y * 16 + lax.rem(owner, 2) * MP + slot
    chosen = jnp.where(column == place, 1.0, 0.0).astype(BF16)
    mine = dot(jnp.concatenate(pieces(pair, 3), axis=0), chosen, (((1,), (0,)), ((), ())))
    pair_high, pair_low = pieces(mine[0:8] + mine[8:16] + mine[16:24], 2)
    unit_high, unit_low = pieces(unit, 2)
    text_grad = dot(
        jnp.concatenate([pair_high, pair_high, pair_low], axis=0),
        jnp.concatenate([unit_high, unit_low, unit_high], axis=0),
        FIRST,
    )
    text_ref[...] = jnp.zeros_like(text_ref)
    for i in range(12):
        text_ref[pl.ds(i, DP, stride=16), :] = text_grad[0:DP, i * 128:(i + 1) * 128]
    attend = dot(resid, wo_ref[...], LAST).astype(BF16)
    wide_attend = attend.astype(F32)
    lane = lanes((64, WIDTH))
    slim = lanes((64, 64))
    for b in range(IMG):
        rows = slice(b * 64, (b + 1) * 64)
        q, k = qkv_ref[0, rows, :], qkv_ref[1, rows, :]
        product = qkv_ref[2, rows, :].astype(F32) * wide_attend[b:b + 1, :]
        query_grad, key_grad, factor = [], [], jnp.zeros((64, 64), F32)
        for h in range(2):
            inside = lane < DH if h == 0 else lane >= DH
            prob_grad = jnp.sum(jnp.where(inside, product, 0.0), axis=1, keepdims=True)
            probs = probs_ref[b * 2 + h].astype(F32)
            mean = jnp.sum(probs * prob_grad, axis=0, keepdims=True)
            score_grad = (probs * (prob_grad - mean) * SCALE).astype(BF16)
            query_grad.append(dot(score_grad, k, FIRST))
            key_grad.append(dot(score_grad, q, (((1,), (0,)), ((), ()))))
            column = jnp.sum(probs, axis=1, keepdims=True)
            factor = factor + jnp.where(slim == h * 8 + b, column, 0.0)
        query_grad = jnp.where(lane < DH, query_grad[0], query_grad[1])
        key_grad = jnp.where(lane < DH, key_grad[0], key_grad[1])
        first = jnp.where(core == 0, factor, 0.0)
        full = jnp.concatenate([query_grad, first, key_grad, factor - first], axis=1)
        for s in range(MP):
            grad_ref[(s * 8 + b) * 8:(s * 8 + b) * 8 + 8, :] = full[s * 8:s * 8 + 8, :]
    turn_ref[...] = jnp.zeros_like(turn_ref)
    start = pl.multiple_of(core * 128, 128)
    for h in range(2):
        part = slice(h * DH, (h + 1) * DH)
        turn_ref[pl.ds(start + 96 + h * 8, 8), 0:DH] = wide_attend[:, part]
        turn_ref[pl.ds(start + 112 + h * 8, 8), 0:DH] = att_ref[:, part]
    turned = [turn_ref[i * 128:(i + 1) * 128, :].T[0:DH, :] for i in range(2)]
    place = lanes((IMG, 512)) - lax.broadcasted_iota(jnp.int32, (IMG, 512), 0) - core * 256
    spot = jnp.where((place == 208) | (place == 216), 1.0, 0.0).astype(BF16)
    normed = jnp.concatenate([r[0:64, :] for r in shards], axis=0)
    grads = grad_ref[...].astype(BF16)
    for c in range(4):
        columns = slice(c * 384, (c + 1) * 384)
        y = dot(normed[:, columns], grads, FIRST) + dot(resid[:, columns], spot, FIRST)
        for j in range(4):
            d = c * 4 + j
            for i in range(4):
                block = y[j * 96:(j + 1) * 96, i * 128:(i + 1) * 128]
                if i % 2 == 1:
                    block = block + turned[i // 2]
                both_ref[d % 2, d // 2, i * 96:(i + 1) * 96, :] = block.astype(BF16)
            both_ref[d % 2, d // 2, 384:400, :] = text_ref[d * 16:(d + 1) * 16, :].astype(BF16)
    keep_ref[...] = both_ref[core]
    give_ref[...] = both_ref[1 - core]


def finish_kernel(r_ref, text_ref, gain_ref, text_out, qkv_out, out_out, stack_ref, line_ref):
    total = r_ref[0].astype(F32)
    for s in range(1, 8):
        total = total + r_ref[s].astype(F32)
    unit_grad = total[384:396, :]
    for i in range(12):
        line_ref[i:i + 1, :] = text_ref[:, i * 128:(i + 1) * 128].astype(F32)
    text = line_ref[...]
    inv = lax.rsqrt(jnp.sum(text * text, keepdims=True) + EPS)
    unit = text * inv
    line_ref[...] = (unit_grad - unit * jnp.sum(unit * unit_grad, keepdims=True)) * inv
    for i in range(12):
        text_out[:, i * 128:(i + 1) * 128] = line_ref[i:i + 1, :]
    first = lax.axis_index("dp") * 96
    shift = lax.rem(first, 128)
    above = gain_ref[pl.ds(lax.div(first, 128), 1), :]
    below = gain_ref[pl.ds(jnp.minimum(lax.div(first, 128) + 1, 11), 1), :]
    gain = jnp.where(lanes((1, 128)) < shift, below, above)
    gain = pltpu.roll(gain, lax.rem(128 - shift, 128), axis=1)[:, 0:96]
    pad = jnp.zeros((32, 128), F32)
    for c in range(2):
        for i in range(2):
            at = (c * 2 + i) * 96
            turned = jnp.concatenate([total[at:at + 96, :], pad], axis=0).T
            rows = 128 if i == 0 else 64
            qkv_out[c, i * 128:i * 128 + rows, :] = turned[0:rows, 0:96] * gain
    lane = lanes((96, 128))
    group = lax.shift_right_logical(lane, 3) - 8
    factors = []
    for s in range(8):
        for c in range(2):
            block = r_ref[s, (c * 2 + 1) * 96:(c * 2 + 2) * 96, :]
            factors.append(block)
            rolled = pltpu.roll(block.astype(F32), 96, axis=1).astype(BF16)
            for g in range(4):
                at = (s * 2 + c) * 128
                stack_ref[g * 96:(g + 1) * 96, at:at + 128] = jnp.where(
                    group == g, rolled, jnp.zeros_like(rolled)
                )
    product = dot(stack_ref[...], jnp.concatenate(factors, axis=1), LAST)
    qkv_out[2] = product[0:192, :] * gain
    out_out[...] = product[192:384, :]


HERE = pl.BlockSpec(memory_space=pltpu.VMEM)
ANY = pl.BlockSpec(memory_space=pl.ANY)
SMEM = pl.BlockSpec(memory_space=pltpu.SMEM)


def call(kernel, outs, scratch, *args, specs=None, params=PARAMS):
    return pl.pallas_call(
        kernel,
        out_shape=[jax.ShapeDtypeStruct(*o) for o in outs],
        in_specs=specs or [HERE] * len(args),
        out_specs=[HERE] * len(outs),
        scratch_shapes=[pltpu.VMEM(*s) if isinstance(s, tuple) else s for s in scratch],
        compiler_params=params,
    )(*args)


def over_mp(block, dz, dy):
    route = [(i, ((i // 2 + dz) % 4) * 2 + (i % 2 + dy) % 2) for i in range(MP)]
    return lax.ppermute(block, "mp", route)


def over_dp(block, dy, dx, dc):
    route = [
        (i, ((i // 8 + dy) % 2 * 4 + (i // 2 + dx) % 4) * 2 + (i + dc) % 2) for i in range(DP)
    ]
    return lax.ppermute(block, "dp", route)


def first_step(block):
    far = over_mp(block, 2, 0)
    across, ahead, behind = [over_mp(block, dz, dy) for dz, dy in STEPS[1:4]]
    return [block, across, ahead, behind, far]


def second_step(blocks):
    across, far = blocks[1], blocks[4]
    return [over_mp(across, 1, 0), over_mp(across, 3, 0), over_mp(far, 0, 1)]


def body(tokens, norm_gain, qkv_weight, out_weight, text_embed, log_temp, logit_bias):
    own, token_sum = call(
        norm_kernel,
        [((72, D), BF16), ((IMG, D), F32)],
        [((12 * 64, 128), F32)],
        tokens,
    )
    own = lax.dynamic_update_slice(own, text_embed, (64, 0))
    own = lax.dynamic_update_slice(own, over_dp(text_embed, 0, 0, 1), (65, 0))
    shards = first_step(own)
    own, qkv_weight, out_weight, gain = lax.optimization_barrier(
        (own, qkv_weight, out_weight, norm_gain)
    )
    qkv_weight, out_weight = call(
        load_kernel,
        [((3, WIDTH, D), BF16), ((WIDTH, D), BF16)],
        [((3, WIDTH, D), BF16), pltpu.SemaphoreType.DMA((2,))],
        qkv_weight, out_weight, gain.reshape(12, 128), specs=[ANY, ANY, HERE],
    )
    shards[1], qkv_weight, out_weight = lax.optimization_barrier(
        (shards[1], qkv_weight, out_weight)
    )
    shards += second_step(shards)
    shards[2], log_temp, logit_bias = lax.optimization_barrier((shards[2], log_temp, logit_bias))
    scalars, = call(scalar_kernel, [((2, 128), F32)], [], log_temp, logit_bias, specs=[SMEM] * 2)
    shards[0], scalars = lax.optimization_barrier((shards[0], scalars))
    early, = call(
        early_kernel, [((3, 320, WIDTH), BF16)], [((320, WIDTH), F32)], *shards[:5], qkv_weight
    )
    shards[0], early = lax.optimization_barrier((shards[0], early))
    kept, = call(
        functools.partial(text_kernel, 0, 7), [((16, D), F32)], [], *shards[:7],
        jnp.zeros((16, D), F32),
    )
    texts, = call(functools.partial(text_kernel, 7, 1), [((16, D), BF16)], [], shards[7], kept)
    texts = [texts, over_dp(texts, 1, 0, 0)]
    part, qkv, probs, attended = call(
        forward_kernel,
        [
            ((MP, IMG, D), BF16), ((3, 512, WIDTH), BF16),
            ((16, 64, 64), BF16), ((IMG, WIDTH), F32),
        ],
        [((192, WIDTH), F32)],
        *shards[5:], early, qkv_weight, out_weight, token_sum,
    )
    part, *texts = lax.optimization_barrier((part, *texts))
    texts = jnp.concatenate(texts + texts, axis=0)
    texts = [texts] + [over_dp(texts, 0, dx, 0) for dx in (1, 2, 3)]
    parts = lax.all_to_all(part, "mp", 0, 0)
    keep, give = call(
        backward_kernel,
        [((8, ROWS, 128), BF16)] * 2,
        [((512, 512), F32), ((256, 128), F32), ((256, 128), F32), ((2, 8, ROWS, 128), BF16)],
        *shards, *texts, parts, qkv, probs, attended, scalars, out_weight,
    )
    other = lax.ppermute(give, "dp", [(i, i ^ 1) for i in range(DP)])
    send = (keep.astype(F32) + other.astype(F32)).astype(BF16)
    received = lax.all_to_all(
        send, "dp", 0, 0, axis_index_groups=[list(range(c, DP, 2)) for c in range(2)]
    )
    text_grad, qkv_grad, out_grad = call(
        finish_kernel,
        [((1, D), F32), ((3, WIDTH, 96), F32), ((WIDTH, 96), F32)],
        [((384, 2048), BF16), ((12, 128), F32)],
        received, text_embed, norm_gain.reshape(12, 128),
    )
    return (text_grad, qkv_grad, out_grad)


def solution(mesh):
    placed = (
        P("dp", "mp"),
        P(),
        P(None, "mp", None),
        P("mp", None),
        P(("dp", "mp"), None),
        P(),
        P(),
    )
    return jax.shard_map(
        body,
        mesh=mesh,
        in_specs=placed,
        out_specs=(P(("dp", "mp"), None), P(None, "mp", "dp"), P("mp", "dp")),
        check_vma=False,
    )
```

```python
import functools
import math

import jax
import jax.numpy as jnp
from jax import lax
from jax.experimental import pallas as pl
from jax.experimental.pallas import tpu as pltpu
from jax.sharding import PartitionSpec as P

D = 1536
DH = 96
TOK = 64
IMG = 8
MP = 8
DP = 16
TEXT = DP * MP
WIDTH = 192
EPS = 1e-06
F32 = jnp.float32
BF16 = jnp.bfloat16
SCALE = 1.0 / math.sqrt(DH)
ROWS = 400
LAST = (((1,), (1,)), ((), ()))
FIRST = (((0,), (0,)), ((), ()))
PARAMS = pltpu.CompilerParams(vmem_limit_bytes=48 * 1024 * 1024)


def dot(a, b, dims):
    return lax.dot_general(a, b, dims, preferred_element_type=F32)


def pieces(a, n):
    out = []
    for _ in range(n):
        p = a.astype(BF16)
        out.append(p)
        a = a - p.astype(F32)
    return out


def lanes(shape):
    return lax.broadcasted_iota(jnp.int32, shape, len(shape) - 1)


def norm_kernel(tok_ref, out_ref, sum_ref, rows_ref):
    total = jnp.zeros((IMG, D), F32)
    for t in range(8):
        x = tok_ref[:, t * D:(t + 1) * D].astype(F32)
        center = x - jnp.mean(x, axis=-1, keepdims=True)
        spread = jnp.mean(center * center, axis=-1, keepdims=True)
        row = center * lax.rsqrt(spread + EPS)
        for i in range(12):
            rows_ref[pl.ds(i * 64 + t, IMG, stride=8), :] = row[:, i * 128:(i + 1) * 128]
        total = total + x
    sum_ref[...] = total
    out_ref[0:64, :] = jnp.concatenate(
        [rows_ref[i * 64:(i + 1) * 64, :] for i in range(12)], axis=1
    ).astype(BF16)
    out_ref[64:72, :] = jnp.zeros((8, D), BF16)


def scalar_kernel(temp_ref, bias_ref, scalar_ref):
    scalar_ref[0:1, :] = jnp.exp(jnp.full((1, 128), temp_ref[0], F32))
    scalar_ref[1:2, :] = jnp.full((1, 128), bias_ref[0], F32)


STEPS = ((0, 0), (0, 1), (1, 0), (3, 0), (2, 0), (1, 1), (3, 1), (2, 1))


def source(slot, step):
    dz, dy = STEPS[step]
    return lax.rem(lax.div(slot, 2) + 4 - dz, 4) * 2 + lax.rem(lax.rem(slot, 2) + dy, 2)


def text_kernel(first, count, *refs):
    shards, (kept_ref, out_ref) = refs[:count], refs[count:]
    slot = lax.axis_index("mp")
    core = lax.rem(lax.axis_index("dp"), 2)
    row = lax.broadcasted_iota(jnp.int32, (16, D), 0)
    total = kept_ref[...]
    for s in range(count):
        two = shards[s][64:72, :].astype(F32)
        for i in range(2):
            at = lax.rem(core + i, 2) * 8 + source(slot, first + s)
            total = jnp.where(row == at, two[i:i + 1, :], total)
    out_ref[...] = total.astype(out_ref.dtype)


def early_kernel(*refs):
    shards, (raw_ref, gain_ref, qkv_ref, w_ref, wide_ref) = refs[:5], refs[5:]
    for i in range(12):
        part = slice(i * 128, (i + 1) * 128)
        for c in range(3):
            scaled = raw_ref[c, :, part].astype(F32) * gain_ref[i:i + 1, :]
            w_ref[c, :, part] = scaled.astype(BF16)
    normed = jnp.concatenate([r[0:64, :] for r in shards], axis=0)
    for c in range(3):
        wide_ref[...] = dot(normed, w_ref[c], LAST)
        for b in range(IMG):
            block = jnp.concatenate(
                [wide_ref[(s * 8 + b) * 8:(s * 8 + b) * 8 + 8, :] for s in range(5)], axis=0
            )
            qkv_ref[c, b * 40:(b + 1) * 40, :] = block.astype(BF16)


def forward_kernel(*refs):
    shards, (early_ref, w_ref, wo_ref, sum_ref), refs = refs[:3], refs[3:7], refs[7:]
    part_ref, qkv_ref, att_ref, wide_ref = refs
    normed = jnp.concatenate([r[0:64, :] for r in shards], axis=0)
    for c in range(3):
        wide_ref[...] = dot(normed, w_ref[c], LAST)
        for b in range(IMG):
            block = jnp.concatenate(
                [early_ref[c, b * 40:(b + 1) * 40, :].astype(F32)]
                + [wide_ref[(s * 8 + b) * 8:(s * 8 + b) * 8 + 8, :] for s in range(3)], axis=0
            )
            qkv_ref[c, b * 64:(b + 1) * 64, 0:WIDTH] = block.astype(BF16)
    lane = lanes((64, WIDTH))
    for b in range(IMG):
        rows = slice(b * 64, (b + 1) * 64)
        q, k = qkv_ref[0, rows, 0:WIDTH], qkv_ref[1, rows, 0:WIDTH]
        v = qkv_ref[2, rows, 0:WIDTH].astype(F32)
        columns = []
        for h in range(2):
            inside = lane < DH if h == 0 else lane >= DH
            score = dot(k, jnp.where(inside, q, jnp.zeros_like(q)), LAST) * SCALE
            weights = jnp.exp(score)
            probs = (weights / jnp.sum(weights, axis=0, keepdims=True)).astype(BF16)
            qkv_ref[h, rows, WIDTH:256] = probs
            columns.append(jnp.sum(probs.astype(F32), axis=1, keepdims=True))
        attended = jnp.sum(jnp.where(lane < DH, columns[0], columns[1]) * v, axis=0, keepdims=True)
        att_ref[b:b + 1, :] = attended
    high, low = pieces(att_ref[...], 2)
    branch = dot(jnp.concatenate([high, low], axis=0), wo_ref[...], (((1,), (0,)), ((), ())))
    part = ((branch[0:8] + branch[8:16] + sum_ref[...]) * (1.0 / TOK)).astype(BF16)
    for d in range(MP):
        part_ref[d] = part


def join_kernel(*refs):
    refs[-1][...] = jnp.concatenate([r[...] for r in refs[:-1]], axis=0)


def backward_kernel(*refs):
    shards, t_ref, refs = refs[:MP], refs[MP], refs[MP + 1:]
    part_ref, qkv_ref, att_ref, scalar_ref, wo_ref = refs[:5]
    keep_ref, give_ref, grad_ref, turn_ref, text_ref, both_ref = refs[5:]
    me = lax.axis_index("dp")
    slot = lax.axis_index("mp")
    core = lax.rem(me, 2)
    pooled = jnp.zeros((IMG, D), F32)
    for s in range(MP):
        pooled = pooled + part_ref[s].astype(F32)
    scale = scalar_ref[0:1, :]
    image_inv = lax.rsqrt(jnp.sum(pooled * pooled, axis=-1, keepdims=True) + EPS)
    unit = pooled * image_inv
    text = t_ref[...]
    wide_text = text.astype(F32)
    square = pieces(wide_text * wide_text, 2)
    ones = jnp.ones((IMG, D), BF16)
    text_inv = lax.rsqrt(dot(ones, square[0], LAST) + dot(ones, square[1], LAST) + EPS)
    cosine = dot(jnp.concatenate(pieces(unit, 3), axis=0), text, LAST)
    cosine = (cosine[0:8] + cosine[8:16] + cosine[16:24]) * text_inv
    logits = scale * cosine + scalar_ref[1:2, :]
    image_row = lax.broadcasted_iota(jnp.int32, (IMG, TEXT), 0)
    own = lanes((IMG, TEXT)) == core * MP + image_row
    pair = scale * (jax.nn.sigmoid(logits) - jnp.where(own, 1.0, 0.0))
    unit_grad = dot(
        jnp.concatenate(pieces(pair * text_inv, 3), axis=0), text, (((1,), (0,)), ((), ()))
    )
    unit_grad = unit_grad[0:8] + unit_grad[8:16] + unit_grad[16:24]
    pooled_grad = (unit_grad - unit * jnp.sum(unit * unit_grad, axis=-1, keepdims=True)) * image_inv
    resid = (pooled_grad * (1.0 / TOK)).astype(BF16)
    column = lax.broadcasted_iota(jnp.int32, (TEXT, DP), 0)
    owner = lanes((TEXT, DP))
    step_x = lax.rem(lax.rem(lax.div(me, 2), 4) - lax.rem(lax.div(owner, 2), 4) + 4, 4)
    step_y = lax.rem(lax.div(me, 8) + lax.div(owner, 8), 2)
    place = step_x * 32 + step_y * 16 + lax.rem(owner, 2) * MP + slot
    chosen = jnp.where(column == place, 1.0, 0.0).astype(BF16)
    mine = dot(jnp.concatenate(pieces(pair, 3), axis=0), chosen, (((1,), (0,)), ((), ())))
    pair_high, pair_low = pieces(mine[0:8] + mine[8:16] + mine[16:24], 2)
    unit_high, unit_low = pieces(unit, 2)
    text_grad = dot(
        jnp.concatenate([pair_high, pair_high, pair_low], axis=0),
        jnp.concatenate([unit_high, unit_low, unit_high], axis=0),
        FIRST,
    )
    text_ref[...] = jnp.zeros_like(text_ref)
    for i in range(12):
        text_ref[pl.ds(i, DP, stride=16), :] = text_grad[0:DP, i * 128:(i + 1) * 128]
    attend = dot(resid, wo_ref[...], LAST).astype(BF16)
    wide_attend = attend.astype(F32)
    lane = lanes((64, WIDTH))
    slim = lanes((64, 64))
    for b in range(IMG):
        rows = slice(b * 64, (b + 1) * 64)
        q, k = qkv_ref[0, rows, 0:WIDTH], qkv_ref[1, rows, 0:WIDTH]
        product = qkv_ref[2, rows, 0:WIDTH].astype(F32) * wide_attend[b:b + 1, :]
        query_grad, key_grad, factor = [], [], jnp.zeros((64, 64), F32)
        for h in range(2):
            inside = lane < DH if h == 0 else lane >= DH
            prob_grad = jnp.sum(jnp.where(inside, product, 0.0), axis=1, keepdims=True)
            probs = qkv_ref[h, rows, WIDTH:256].astype(F32)
            mean = jnp.sum(probs * prob_grad, axis=0, keepdims=True)
            score_grad = (probs * (prob_grad - mean) * SCALE).astype(BF16)
            query_grad.append(dot(score_grad, k, FIRST))
            key_grad.append(dot(score_grad, q, (((1,), (0,)), ((), ()))))
            column = jnp.sum(probs, axis=1, keepdims=True)
            factor = factor + jnp.where(slim == h * 8 + b, column, 0.0)
        query_grad = jnp.where(lane < DH, query_grad[0], query_grad[1])
        key_grad = jnp.where(lane < DH, key_grad[0], key_grad[1])
        first = jnp.where(core == 0, factor, 0.0)
        full = jnp.concatenate([query_grad, first, key_grad, factor - first], axis=1)
        for s in range(MP):
            grad_ref[(s * 8 + b) * 8:(s * 8 + b) * 8 + 8, :] = full[s * 8:s * 8 + 8, :]
    turn_ref[...] = jnp.zeros_like(turn_ref)
    start = pl.multiple_of(core * 128, 128)
    for h in range(2):
        part = slice(h * DH, (h + 1) * DH)
        turn_ref[pl.ds(start + 96 + h * 8, 8), 0:DH] = wide_attend[:, part]
        turn_ref[pl.ds(start + 112 + h * 8, 8), 0:DH] = att_ref[:, part]
    turned = [turn_ref[i * 128:(i + 1) * 128, :].T[0:DH, :] for i in range(2)]
    place = lanes((IMG, 512)) - lax.broadcasted_iota(jnp.int32, (IMG, 512), 0) - core * 256
    spot = jnp.where((place == 208) | (place == 216), 1.0, 0.0).astype(BF16)
    normed = jnp.concatenate([r[0:64, :] for r in shards], axis=0)
    grads = grad_ref[...].astype(BF16)
    for c in range(4):
        columns = slice(c * 384, (c + 1) * 384)
        y = dot(normed[:, columns], grads, FIRST) + dot(resid[:, columns], spot, FIRST)
        for j in range(4):
            d = c * 4 + j
            for i in range(4):
                block = y[j * 96:(j + 1) * 96, i * 128:(i + 1) * 128]
                if i % 2 == 1:
                    block = block + turned[i // 2]
                both_ref[d % 2, d // 2, i * 96:(i + 1) * 96, :] = block.astype(BF16)
            both_ref[d % 2, d // 2, 384:400, :] = text_ref[d * 16:(d + 1) * 16, :].astype(BF16)
    keep_ref[...] = both_ref[core]
    give_ref[...] = both_ref[1 - core]


def finish_kernel(r_ref, text_ref, gain_ref, text_out, qkv_out, out_out, stack_ref, line_ref):
    total = r_ref[0].astype(F32)
    for s in range(1, 8):
        total = total + r_ref[s].astype(F32)
    unit_grad = total[384:396, :]
    for i in range(12):
        line_ref[i:i + 1, :] = text_ref[:, i * 128:(i + 1) * 128].astype(F32)
    text = line_ref[...]
    inv = lax.rsqrt(jnp.sum(text * text, keepdims=True) + EPS)
    unit = text * inv
    line_ref[...] = (unit_grad - unit * jnp.sum(unit * unit_grad, keepdims=True)) * inv
    for i in range(12):
        text_out[:, i * 128:(i + 1) * 128] = line_ref[i:i + 1, :]
    first = lax.axis_index("dp") * 96
    shift = lax.rem(first, 128)
    above = gain_ref[pl.ds(lax.div(first, 128), 1), :]
    below = gain_ref[pl.ds(jnp.minimum(lax.div(first, 128) + 1, 11), 1), :]
    gain = jnp.where(lanes((1, 128)) < shift, below, above)
    gain = pltpu.roll(gain, lax.rem(128 - shift, 128), axis=1)[:, 0:96]
    pad = jnp.zeros((32, 128), F32)
    for c in range(2):
        for i in range(2):
            at = (c * 2 + i) * 96
            turned = jnp.concatenate([total[at:at + 96, :], pad], axis=0).T
            rows = 128 if i == 0 else 64
            qkv_out[c, i * 128:i * 128 + rows, :] = turned[0:rows, 0:96] * gain
    lane = lanes((96, 128))
    group = lax.shift_right_logical(lane, 3) - 8
    factors = []
    for s in range(8):
        for c in range(2):
            block = r_ref[s, (c * 2 + 1) * 96:(c * 2 + 2) * 96, :]
            factors.append(block)
            rolled = pltpu.roll(block.astype(F32), 96, axis=1).astype(BF16)
            for g in range(4):
                at = (s * 2 + c) * 128
                stack_ref[g * 96:(g + 1) * 96, at:at + 128] = jnp.where(
                    group == g, rolled, jnp.zeros_like(rolled)
                )
    product = dot(stack_ref[...], jnp.concatenate(factors, axis=1), LAST)
    qkv_out[2] = product[0:192, :] * gain
    out_out[...] = product[192:384, :]


HERE = pl.BlockSpec(memory_space=pltpu.VMEM)
ANY = pl.BlockSpec(memory_space=pl.ANY)
SMEM = pl.BlockSpec(memory_space=pltpu.SMEM)


def call(kernel, outs, scratch, *args, specs=None, params=PARAMS):
    return pl.pallas_call(
        kernel,
        out_shape=[jax.ShapeDtypeStruct(*o) for o in outs],
        in_specs=specs or [HERE] * len(args),
        out_specs=[HERE] * len(outs),
        scratch_shapes=[pltpu.VMEM(*s) if isinstance(s, tuple) else s for s in scratch],
        compiler_params=params,
    )(*args)


def over_mp(block, dz, dy):
    route = [(i, ((i // 2 + dz) % 4) * 2 + (i % 2 + dy) % 2) for i in range(MP)]
    return lax.ppermute(block, "mp", route)


def over_dp(block, dy, dx, dc):
    route = [
        (i, ((i // 8 + dy) % 2 * 4 + (i // 2 + dx) % 4) * 2 + (i + dc) % 2) for i in range(DP)
    ]
    return lax.ppermute(block, "dp", route)


def first_step(block):
    far = over_mp(block, 2, 0)
    across, ahead, behind = [over_mp(block, dz, dy) for dz, dy in STEPS[1:4]]
    return [block, across, ahead, behind, far]


def second_step(blocks):
    across, far = blocks[1], blocks[4]
    return [over_mp(across, 1, 0), over_mp(across, 3, 0), over_mp(far, 0, 1)]


def body(tokens, norm_gain, qkv_weight, out_weight, text_embed, log_temp, logit_bias):
    own, token_sum = call(
        norm_kernel,
        [((72, D), BF16), ((IMG, D), F32)],
        [((12 * 64, 128), F32)],
        tokens,
    )
    own = lax.dynamic_update_slice(own, text_embed, (64, 0))
    own = lax.dynamic_update_slice(own, over_dp(text_embed, 0, 0, 1), (65, 0))
    shards = first_step(own)
    shards += second_step(shards)
    shards[2], log_temp, logit_bias = lax.optimization_barrier((shards[2], log_temp, logit_bias))
    scalars, = call(scalar_kernel, [((2, 128), F32)], [], log_temp, logit_bias, specs=[SMEM] * 2)
    shards[0], scalars = lax.optimization_barrier((shards[0], scalars))
    early, scaled = call(
        early_kernel,
        [((3, 320, WIDTH), BF16), ((3, WIDTH, D), BF16)],
        [((320, WIDTH), F32)],
        *shards[:5], qkv_weight, norm_gain.reshape(12, 128),
    )
    shards[0], early = lax.optimization_barrier((shards[0], early))
    kept, = call(
        functools.partial(text_kernel, 0, 7), [((16, D), F32)], [], *shards[:7],
        jnp.zeros((16, D), F32),
    )
    texts, = call(functools.partial(text_kernel, 7, 1), [((16, D), BF16)], [], shards[7], kept)
    texts = [texts, over_dp(texts, 1, 0, 0)]
    part, qkv, attended = call(
        forward_kernel,
        [
            ((MP, IMG, D), BF16), ((3, 512, 256), BF16), ((IMG, WIDTH), F32),
        ],
        [((192, WIDTH), F32)],
        *shards[5:], early, scaled, out_weight, token_sum,
    )
    texts = jnp.concatenate(texts, axis=0)
    texts = [texts] + [over_dp(texts, 0, dx, 0) for dx in (1, 2, 3)]
    parts = lax.all_to_all(part, "mp", 0, 0)
    texts, = call(join_kernel, [((TEXT, D), BF16)], [], *texts)
    keep, give = call(
        backward_kernel,
        [((8, ROWS, 128), BF16)] * 2,
        [((512, 512), F32), ((256, 128), F32), ((256, 128), F32), ((2, 8, ROWS, 128), BF16)],
        *shards, texts, parts, qkv, attended, scalars, out_weight,
    )
    other = lax.ppermute(give, "dp", [(i, i ^ 1) for i in range(DP)])
    send = (keep.astype(F32) + other.astype(F32)).astype(BF16)
    received = lax.all_to_all(
        send, "dp", 0, 0, axis_index_groups=[list(range(c, DP, 2)) for c in range(2)]
    )
    text_grad, qkv_grad, out_grad = call(
        finish_kernel,
        [((1, D), F32), ((3, WIDTH, 96), F32), ((WIDTH, 96), F32)],
        [((384, 2048), BF16), ((12, 128), F32)],
        received, text_embed, norm_gain.reshape(12, 128),
    )
    return (text_grad, qkv_grad, out_grad)


def solution(mesh):
    placed = (
        P("dp", "mp"),
        P(),
        P(None, "mp", None),
        P("mp", None),
        P(("dp", "mp"), None),
        P(),
        P(),
    )
    return jax.shard_map(
        body,
        mesh=mesh,
        in_specs=placed,
        out_specs=(P(("dp", "mp"), None), P(None, "mp", "dp"), P("mp", "dp")),
        check_vma=False,
    )
```

```python
import functools
import math

import jax
import jax.numpy as jnp
from jax import lax
from jax.experimental import pallas as pl
from jax.experimental.pallas import tpu as pltpu
from jax.sharding import PartitionSpec as P

D = 1536
DH = 96
TOK = 64
IMG = 8
MP = 8
DP = 16
TEXT = DP * MP
WIDTH = 192
EPS = 1e-06
F32 = jnp.float32
BF16 = jnp.bfloat16
SCALE = 1.0 / math.sqrt(DH)
ROWS = 400
LAST = (((1,), (1,)), ((), ()))
FIRST = (((0,), (0,)), ((), ()))
PARAMS = pltpu.CompilerParams(vmem_limit_bytes=48 * 1024 * 1024)


def dot(a, b, dims):
    return lax.dot_general(a, b, dims, preferred_element_type=F32)


def pieces(a, n):
    out = []
    for _ in range(n):
        p = a.astype(BF16)
        out.append(p)
        a = a - p.astype(F32)
    return out


def lanes(shape):
    return lax.broadcasted_iota(jnp.int32, shape, len(shape) - 1)


def norm_kernel(tok_ref, out_ref, sum_ref, rows_ref):
    total = jnp.zeros((IMG, D), F32)
    for t in range(8):
        x = tok_ref[:, t * D:(t + 1) * D].astype(F32)
        center = x - jnp.mean(x, axis=-1, keepdims=True)
        spread = jnp.mean(center * center, axis=-1, keepdims=True)
        row = center * lax.rsqrt(spread + EPS)
        for i in range(12):
            rows_ref[pl.ds(i * 64 + t, IMG, stride=8), :] = row[:, i * 128:(i + 1) * 128]
        total = total + x
    sum_ref[...] = total
    out_ref[0:64, :] = jnp.concatenate(
        [rows_ref[i * 64:(i + 1) * 64, :] for i in range(12)], axis=1
    ).astype(BF16)
    out_ref[64:72, :] = jnp.zeros((8, D), BF16)


def scalar_kernel(temp_ref, bias_ref, scalar_ref):
    scalar_ref[0:1, :] = jnp.exp(jnp.full((1, 128), temp_ref[0], F32))
    scalar_ref[1:2, :] = jnp.full((1, 128), bias_ref[0], F32)


STEPS = ((0, 0), (0, 1), (1, 0), (3, 0), (2, 0), (1, 1), (3, 1), (2, 1))


def source(slot, step):
    dz, dy = STEPS[step]
    return lax.rem(lax.div(slot, 2) + 4 - dz, 4) * 2 + lax.rem(lax.rem(slot, 2) + dy, 2)


def text_kernel(first, count, *refs):
    shards, (kept_ref, out_ref) = refs[:count], refs[count:]
    slot = lax.axis_index("mp")
    core = lax.rem(lax.axis_index("dp"), 2)
    row = lax.broadcasted_iota(jnp.int32, (16, D), 0)
    total = kept_ref[...]
    for s in range(count):
        two = shards[s][64:72, :].astype(F32)
        for i in range(2):
            at = lax.rem(core + i, 2) * 8 + source(slot, first + s)
            total = jnp.where(row == at, two[i:i + 1, :], total)
    out_ref[...] = total.astype(out_ref.dtype)


def early_kernel(*refs):
    shards, (raw_ref, gain_ref, qkv_ref, w_ref, wide_ref) = refs[:5], refs[5:]
    for i in range(12):
        part = slice(i * 128, (i + 1) * 128)
        for c in range(3):
            scaled = raw_ref[c, :, part].astype(F32) * gain_ref[i:i + 1, :]
            w_ref[c, :, part] = scaled.astype(BF16)
    normed = jnp.concatenate([r[0:64, :] for r in shards], axis=0)
    for c in range(3):
        wide_ref[...] = dot(normed, w_ref[c], LAST)
        for b in range(IMG):
            block = jnp.concatenate(
                [wide_ref[(s * 8 + b) * 8:(s * 8 + b) * 8 + 8, :] for s in range(5)], axis=0
            )
            qkv_ref[c, b * 40:(b + 1) * 40, :] = block.astype(BF16)


def forward_kernel(*refs):
    shards, (early_ref, w_ref, wo_ref, sum_ref), refs = refs[:3], refs[3:7], refs[7:]
    part_ref, *qkv_ref, att_ref, wide_ref = refs
    normed = jnp.concatenate([r[0:64, :] for r in shards], axis=0)
    for c in range(3):
        wide_ref[...] = dot(normed, w_ref[c], LAST)
        for b in range(IMG):
            block = jnp.concatenate(
                [early_ref[c, b * 40:(b + 1) * 40, :].astype(F32)]
                + [wide_ref[(s * 8 + b) * 8:(s * 8 + b) * 8 + 8, :] for s in range(3)], axis=0
            )
            qkv_ref[c][b * 64:(b + 1) * 64, 0:WIDTH] = block.astype(BF16)
    lane = lanes((64, WIDTH))
    for b in range(IMG):
        rows = slice(b * 64, (b + 1) * 64)
        q, k = qkv_ref[0][rows, 0:WIDTH], qkv_ref[1][rows, 0:WIDTH]
        v = qkv_ref[2][rows, 0:WIDTH].astype(F32)
        columns = []
        for h in range(2):
            inside = lane < DH if h == 0 else lane >= DH
            score = dot(k, jnp.where(inside, q, jnp.zeros_like(q)), LAST) * SCALE
            weights = jnp.exp(score)
            probs = (weights / jnp.sum(weights, axis=0, keepdims=True)).astype(BF16)
            qkv_ref[h][rows, WIDTH:256] = probs
            columns.append(jnp.sum(probs.astype(F32), axis=1, keepdims=True))
        attended = jnp.sum(jnp.where(lane < DH, columns[0], columns[1]) * v, axis=0, keepdims=True)
        att_ref[b:b + 1, :] = attended
    high, low = pieces(att_ref[...], 2)
    branch = dot(jnp.concatenate([high, low], axis=0), wo_ref[...], (((1,), (0,)), ((), ())))
    part = ((branch[0:8] + branch[8:16] + sum_ref[...]) * (1.0 / TOK)).astype(BF16)
    for d in range(MP):
        part_ref[d] = part


def join_kernel(*refs):
    refs[-1][...] = jnp.concatenate([r[...] for r in refs[:-1]], axis=0)


def backward_kernel(*refs):
    shards, t_ref, refs = refs[:MP], refs[MP], refs[MP + 1:]
    part_ref, *qkv_ref, att_ref, scalar_ref, wo_ref = refs[:7]
    keep_ref, give_ref, grad_ref, turn_ref, text_ref, both_ref = refs[7:]
    me = lax.axis_index("dp")
    slot = lax.axis_index("mp")
    core = lax.rem(me, 2)
    pooled = jnp.zeros((IMG, D), F32)
    for s in range(MP):
        pooled = pooled + part_ref[s].astype(F32)
    scale = scalar_ref[0:1, :]
    image_inv = lax.rsqrt(jnp.sum(pooled * pooled, axis=-1, keepdims=True) + EPS)
    unit = pooled * image_inv
    text = t_ref[...]
    wide_text = text.astype(F32)
    square = pieces(wide_text * wide_text, 2)
    ones = jnp.ones((IMG, D), BF16)
    text_inv = lax.rsqrt(dot(ones, square[0], LAST) + dot(ones, square[1], LAST) + EPS)
    cosine = dot(jnp.concatenate(pieces(unit, 3), axis=0), text, LAST)
    cosine = (cosine[0:8] + cosine[8:16] + cosine[16:24]) * text_inv
    logits = scale * cosine + scalar_ref[1:2, :]
    image_row = lax.broadcasted_iota(jnp.int32, (IMG, TEXT), 0)
    own = lanes((IMG, TEXT)) == core * MP + image_row
    pair = scale * (jax.nn.sigmoid(logits) - jnp.where(own, 1.0, 0.0))
    unit_grad = dot(
        jnp.concatenate(pieces(pair * text_inv, 3), axis=0), text, (((1,), (0,)), ((), ()))
    )
    unit_grad = unit_grad[0:8] + unit_grad[8:16] + unit_grad[16:24]
    pooled_grad = (unit_grad - unit * jnp.sum(unit * unit_grad, axis=-1, keepdims=True)) * image_inv
    resid = (pooled_grad * (1.0 / TOK)).astype(BF16)
    column = lax.broadcasted_iota(jnp.int32, (TEXT, DP), 0)
    owner = lanes((TEXT, DP))
    step_x = lax.rem(lax.rem(lax.div(me, 2), 4) - lax.rem(lax.div(owner, 2), 4) + 4, 4)
    step_y = lax.rem(lax.div(me, 8) + lax.div(owner, 8), 2)
    place = step_x * 32 + step_y * 16 + lax.rem(owner, 2) * MP + slot
    chosen = jnp.where(column == place, 1.0, 0.0).astype(BF16)
    mine = dot(jnp.concatenate(pieces(pair, 3), axis=0), chosen, (((1,), (0,)), ((), ())))
    pair_high, pair_low = pieces(mine[0:8] + mine[8:16] + mine[16:24], 2)
    unit_high, unit_low = pieces(unit, 2)
    text_grad = dot(
        jnp.concatenate([pair_high, pair_high, pair_low], axis=0),
        jnp.concatenate([unit_high, unit_low, unit_high], axis=0),
        FIRST,
    )
    text_ref[...] = jnp.zeros_like(text_ref)
    for i in range(12):
        text_ref[pl.ds(i, DP, stride=16), :] = text_grad[0:DP, i * 128:(i + 1) * 128]
    attend = dot(resid, wo_ref[...], LAST).astype(BF16)
    wide_attend = attend.astype(F32)
    lane = lanes((64, WIDTH))
    slim = lanes((64, 64))
    for b in range(IMG):
        rows = slice(b * 64, (b + 1) * 64)
        q, k = qkv_ref[0][rows, 0:WIDTH], qkv_ref[1][rows, 0:WIDTH]
        product = qkv_ref[2][rows, 0:WIDTH].astype(F32) * wide_attend[b:b + 1, :]
        query_grad, key_grad, factor = [], [], jnp.zeros((64, 64), F32)
        for h in range(2):
            inside = lane < DH if h == 0 else lane >= DH
            prob_grad = jnp.sum(jnp.where(inside, product, 0.0), axis=1, keepdims=True)
            probs = qkv_ref[h][rows, WIDTH:256].astype(F32)
            mean = jnp.sum(probs * prob_grad, axis=0, keepdims=True)
            score_grad = (probs * (prob_grad - mean) * SCALE).astype(BF16)
            query_grad.append(dot(score_grad, k, FIRST))
            key_grad.append(dot(score_grad, q, (((1,), (0,)), ((), ()))))
            column = jnp.sum(probs, axis=1, keepdims=True)
            factor = factor + jnp.where(slim == h * 8 + b, column, 0.0)
        query_grad = jnp.where(lane < DH, query_grad[0], query_grad[1])
        key_grad = jnp.where(lane < DH, key_grad[0], key_grad[1])
        first = jnp.where(core == 0, factor, 0.0)
        full = jnp.concatenate([query_grad, first, key_grad, factor - first], axis=1)
        for s in range(MP):
            grad_ref[(s * 8 + b) * 8:(s * 8 + b) * 8 + 8, :] = full[s * 8:s * 8 + 8, :]
    turn_ref[...] = jnp.zeros_like(turn_ref)
    start = pl.multiple_of(core * 128, 128)
    for h in range(2):
        part = slice(h * DH, (h + 1) * DH)
        turn_ref[pl.ds(start + 96 + h * 8, 8), 0:DH] = wide_attend[:, part]
        turn_ref[pl.ds(start + 112 + h * 8, 8), 0:DH] = att_ref[:, part]
    turned = [turn_ref[i * 128:(i + 1) * 128, :].T[0:DH, :] for i in range(2)]
    place = lanes((IMG, 512)) - lax.broadcasted_iota(jnp.int32, (IMG, 512), 0) - core * 256
    spot = jnp.where((place == 208) | (place == 216), 1.0, 0.0).astype(BF16)
    normed = jnp.concatenate([r[0:64, :] for r in shards], axis=0)
    grads = grad_ref[...].astype(BF16)
    for c in range(4):
        columns = slice(c * 384, (c + 1) * 384)
        y = dot(normed[:, columns], grads, FIRST) + dot(resid[:, columns], spot, FIRST)
        for j in range(4):
            d = c * 4 + j
            for i in range(4):
                block = y[j * 96:(j + 1) * 96, i * 128:(i + 1) * 128]
                if i % 2 == 1:
                    block = block + turned[i // 2]
                both_ref[d % 2, d // 2, i * 96:(i + 1) * 96, :] = block.astype(BF16)
            both_ref[d % 2, d // 2, 384:400, :] = text_ref[d * 16:(d + 1) * 16, :].astype(BF16)
    keep_ref[...] = both_ref[core]
    give_ref[...] = both_ref[1 - core]


def finish_kernel(r_ref, text_ref, gain_ref, text_out, qkv_out, out_out, stack_ref, line_ref):
    total = r_ref[0].astype(F32)
    for s in range(1, 8):
        total = total + r_ref[s].astype(F32)
    unit_grad = total[384:396, :]
    for i in range(12):
        line_ref[i:i + 1, :] = text_ref[:, i * 128:(i + 1) * 128].astype(F32)
    text = line_ref[...]
    inv = lax.rsqrt(jnp.sum(text * text, keepdims=True) + EPS)
    unit = text * inv
    line_ref[...] = (unit_grad - unit * jnp.sum(unit * unit_grad, keepdims=True)) * inv
    for i in range(12):
        text_out[:, i * 128:(i + 1) * 128] = line_ref[i:i + 1, :]
    first = lax.axis_index("dp") * 96
    shift = lax.rem(first, 128)
    above = gain_ref[pl.ds(lax.div(first, 128), 1), :]
    below = gain_ref[pl.ds(jnp.minimum(lax.div(first, 128) + 1, 11), 1), :]
    gain = jnp.where(lanes((1, 128)) < shift, below, above)
    gain = pltpu.roll(gain, lax.rem(128 - shift, 128), axis=1)[:, 0:96]
    pad = jnp.zeros((32, 128), F32)
    for c in range(2):
        for i in range(2):
            at = (c * 2 + i) * 96
            turned = jnp.concatenate([total[at:at + 96, :], pad], axis=0).T
            rows = 128 if i == 0 else 64
            qkv_out[c, i * 128:i * 128 + rows, :] = turned[0:rows, 0:96] * gain
    lane = lanes((96, 128))
    group = lax.shift_right_logical(lane, 3) - 8
    factors = []
    for s in range(8):
        for c in range(2):
            block = r_ref[s, (c * 2 + 1) * 96:(c * 2 + 2) * 96, :]
            factors.append(block)
            rolled = pltpu.roll(block.astype(F32), 96, axis=1).astype(BF16)
            for g in range(4):
                at = (s * 2 + c) * 128
                stack_ref[g * 96:(g + 1) * 96, at:at + 128] = jnp.where(
                    group == g, rolled, jnp.zeros_like(rolled)
                )
    product = dot(stack_ref[...], jnp.concatenate(factors, axis=1), LAST)
    qkv_out[2] = product[0:192, :] * gain
    out_out[...] = product[192:384, :]


HERE = pl.BlockSpec(memory_space=pltpu.VMEM)
ANY = pl.BlockSpec(memory_space=pl.ANY)
SMEM = pl.BlockSpec(memory_space=pltpu.SMEM)


def call(kernel, outs, scratch, *args, specs=None, params=PARAMS):
    return pl.pallas_call(
        kernel,
        out_shape=[jax.ShapeDtypeStruct(*o) for o in outs],
        in_specs=specs or [HERE] * len(args),
        out_specs=[HERE] * len(outs),
        scratch_shapes=[pltpu.VMEM(*s) if isinstance(s, tuple) else s for s in scratch],
        compiler_params=params,
    )(*args)


def over_mp(block, dz, dy):
    route = [(i, ((i // 2 + dz) % 4) * 2 + (i % 2 + dy) % 2) for i in range(MP)]
    return lax.ppermute(block, "mp", route)


def over_dp(block, dy, dx, dc):
    route = [
        (i, ((i // 8 + dy) % 2 * 4 + (i // 2 + dx) % 4) * 2 + (i + dc) % 2) for i in range(DP)
    ]
    return lax.ppermute(block, "dp", route)


def first_step(block):
    far = over_mp(block, 2, 0)
    across, ahead, behind = [over_mp(block, dz, dy) for dz, dy in STEPS[1:4]]
    return [block, across, ahead, behind, far]


def second_step(blocks):
    across, far = blocks[1], blocks[4]
    return [over_mp(across, 1, 0), over_mp(across, 3, 0), over_mp(far, 0, 1)]


def body(tokens, norm_gain, qkv_weight, out_weight, text_embed, log_temp, logit_bias):
    own, token_sum = call(
        norm_kernel,
        [((72, D), BF16), ((IMG, D), F32)],
        [((12 * 64, 128), F32)],
        tokens,
    )
    own = lax.dynamic_update_slice(own, text_embed, (64, 0))
    own = lax.dynamic_update_slice(own, over_dp(text_embed, 0, 0, 1), (65, 0))
    shards = first_step(own)
    shards += second_step(shards)
    shards[2], log_temp, logit_bias = lax.optimization_barrier((shards[2], log_temp, logit_bias))
    scalars, = call(scalar_kernel, [((2, 128), F32)], [], log_temp, logit_bias, specs=[SMEM] * 2)
    shards[0], scalars = lax.optimization_barrier((shards[0], scalars))
    early, scaled = call(
        early_kernel,
        [((3, 320, WIDTH), BF16), ((3, WIDTH, D), BF16)],
        [((320, WIDTH), F32)],
        *shards[:5], qkv_weight, norm_gain.reshape(12, 128),
    )
    shards[0], early = lax.optimization_barrier((shards[0], early))
    kept, = call(
        functools.partial(text_kernel, 0, 7), [((16, D), F32)], [], *shards[:7],
        jnp.zeros((16, D), F32),
    )
    texts, = call(functools.partial(text_kernel, 7, 1), [((16, D), BF16)], [], shards[7], kept)
    texts = [texts, over_dp(texts, 1, 0, 0)]
    part, *qkv, attended = call(
        forward_kernel,
        [
            ((MP, IMG, D), BF16), ((512, 256), BF16), ((512, 256), BF16),
            ((512, WIDTH), BF16), ((IMG, WIDTH), F32),
        ],
        [((192, WIDTH), F32)],
        *shards[5:], early, scaled, out_weight, token_sum,
    )
    texts = jnp.concatenate(texts, axis=0)
    texts = [texts] + [over_dp(texts, 0, dx, 0) for dx in (1, 2, 3)]
    parts = lax.all_to_all(part, "mp", 0, 0)
    texts, = call(join_kernel, [((TEXT, D), BF16)], [], *texts)
    keep, give = call(
        backward_kernel,
        [((8, ROWS, 128), BF16)] * 2,
        [((512, 512), F32), ((256, 128), F32), ((256, 128), F32), ((2, 8, ROWS, 128), BF16)],
        *shards, texts, parts, *qkv, attended, scalars, out_weight,
    )
    other = lax.ppermute(give, "dp", [(i, i ^ 1) for i in range(DP)])
    send = (keep.astype(F32) + other.astype(F32)).astype(BF16)
    received = lax.all_to_all(
        send, "dp", 0, 0, axis_index_groups=[list(range(c, DP, 2)) for c in range(2)]
    )
    text_grad, qkv_grad, out_grad = call(
        finish_kernel,
        [((1, D), F32), ((3, WIDTH, 96), F32), ((WIDTH, 96), F32)],
        [((384, 2048), BF16), ((12, 128), F32)],
        received, text_embed, norm_gain.reshape(12, 128),
    )
    return (text_grad, qkv_grad, out_grad)


def solution(mesh):
    placed = (
        P("dp", "mp"),
        P(),
        P(None, "mp", None),
        P("mp", None),
        P(("dp", "mp"), None),
        P(),
        P(),
    )
    return jax.shard_map(
        body,
        mesh=mesh,
        in_specs=placed,
        out_specs=(P(("dp", "mp"), None), P(None, "mp", "dp"), P("mp", "dp")),
        check_vma=False,
    )
```

```python
import functools
import math

import jax
import jax.numpy as jnp
from jax import lax
from jax.experimental import pallas as pl
from jax.experimental.pallas import tpu as pltpu
from jax.sharding import PartitionSpec as P

D = 1536
DH = 96
TOK = 64
IMG = 8
MP = 8
DP = 16
TEXT = DP * MP
WIDTH = 192
EPS = 1e-06
F32 = jnp.float32
BF16 = jnp.bfloat16
SCALE = 1.0 / math.sqrt(DH)
ROWS = 400
LAST = (((1,), (1,)), ((), ()))
FIRST = (((0,), (0,)), ((), ()))
PARAMS = pltpu.CompilerParams(vmem_limit_bytes=48 * 1024 * 1024)


def dot(a, b, dims):
    return lax.dot_general(a, b, dims, preferred_element_type=F32)


def pieces(a, n):
    out = []
    for _ in range(n):
        p = a.astype(BF16)
        out.append(p)
        a = a - p.astype(F32)
    return out


def lanes(shape):
    return lax.broadcasted_iota(jnp.int32, shape, len(shape) - 1)


def norm_kernel(tok_ref, out_ref, sum_ref, rows_ref):
    total = jnp.zeros((IMG, D), F32)
    for t in range(8):
        x = tok_ref[:, t * D:(t + 1) * D].astype(F32)
        center = x - jnp.mean(x, axis=-1, keepdims=True)
        spread = jnp.mean(center * center, axis=-1, keepdims=True)
        row = center * lax.rsqrt(spread + EPS)
        for i in range(12):
            rows_ref[pl.ds(i * 64 + t, IMG, stride=8), :] = row[:, i * 128:(i + 1) * 128]
        total = total + x
    sum_ref[...] = total
    out_ref[0:64, :] = jnp.concatenate(
        [rows_ref[i * 64:(i + 1) * 64, :] for i in range(12)], axis=1
    ).astype(BF16)
    out_ref[64:72, :] = jnp.zeros((8, D), BF16)


def scalar_kernel(temp_ref, bias_ref, scalar_ref):
    scalar_ref[0:1, :] = jnp.exp(jnp.full((1, 128), temp_ref[0], F32))
    scalar_ref[1:2, :] = jnp.full((1, 128), bias_ref[0], F32)


STEPS = ((0, 0), (0, 1), (1, 0), (3, 0), (2, 0), (1, 1), (3, 1), (2, 1))


def source(slot, step):
    dz, dy = STEPS[step]
    return lax.rem(lax.div(slot, 2) + 4 - dz, 4) * 2 + lax.rem(lax.rem(slot, 2) + dy, 2)


def text_kernel(first, count, *refs):
    shards, (kept_ref, out_ref) = refs[:count], refs[count:]
    slot = lax.axis_index("mp")
    core = lax.rem(lax.axis_index("dp"), 2)
    row = lax.broadcasted_iota(jnp.int32, (16, D), 0)
    total = kept_ref[...]
    for s in range(count):
        two = shards[s][64:72, :].astype(F32)
        for i in range(2):
            at = lax.rem(core + i, 2) * 8 + source(slot, first + s)
            total = jnp.where(row == at, two[i:i + 1, :], total)
    out_ref[...] = total.astype(out_ref.dtype)


def early_kernel(*refs):
    shards, (raw_ref, gain_ref, qkv_ref, w_ref, wide_ref) = refs[:5], refs[5:]
    for i in range(12):
        part = slice(i * 128, (i + 1) * 128)
        for c in range(3):
            scaled = raw_ref[c, :, part].astype(F32) * gain_ref[i:i + 1, :]
            w_ref[c, :, part] = scaled.astype(BF16)
    normed = jnp.concatenate([r[0:64, :] for r in shards], axis=0)
    for c in range(3):
        wide_ref[...] = dot(normed, w_ref[c], LAST)
        for b in range(IMG):
            block = jnp.concatenate(
                [wide_ref[(s * 8 + b) * 8:(s * 8 + b) * 8 + 8, :] for s in range(5)], axis=0
            )
            qkv_ref[c, b * 40:(b + 1) * 40, :] = block.astype(BF16)


def forward_kernel(*refs):
    shards, (early_ref, w_ref, wo_ref, sum_ref), refs = refs[:3], refs[3:7], refs[7:]
    part_ref, *qkv_ref, att_ref, wide_ref = refs
    normed = jnp.concatenate([r[0:64, :] for r in shards], axis=0)
    for c in range(3):
        wide_ref[...] = dot(normed, w_ref[c], LAST)
        for b in range(IMG):
            block = jnp.concatenate(
                [early_ref[c, b * 40:(b + 1) * 40, :].astype(F32)]
                + [wide_ref[(s * 8 + b) * 8:(s * 8 + b) * 8 + 8, :] for s in range(3)], axis=0
            )
            qkv_ref[c][b * 64:(b + 1) * 64, 0:WIDTH] = block.astype(BF16)
    lane = lanes((64, WIDTH))
    for b in range(IMG):
        rows = slice(b * 64, (b + 1) * 64)
        q, k = qkv_ref[0][rows, 0:WIDTH], qkv_ref[1][rows, 0:WIDTH]
        v = qkv_ref[2][rows, 0:WIDTH].astype(F32)
        columns = []
        for h in range(2):
            inside = lane < DH if h == 0 else lane >= DH
            score = dot(k, jnp.where(inside, q, jnp.zeros_like(q)), LAST) * SCALE
            weights = jnp.exp(score)
            probs = (weights / jnp.sum(weights, axis=0, keepdims=True)).astype(BF16)
            qkv_ref[h][rows, WIDTH:256] = probs
            columns.append(jnp.sum(probs.astype(F32), axis=1, keepdims=True))
        attended = jnp.sum(jnp.where(lane < DH, columns[0], columns[1]) * v, axis=0, keepdims=True)
        att_ref[b:b + 1, :] = attended
    high, low = pieces(att_ref[...], 2)
    branch = dot(jnp.concatenate([high, low], axis=0), wo_ref[...], (((1,), (0,)), ((), ())))
    part = ((branch[0:8] + branch[8:16] + sum_ref[...]) * (1.0 / TOK)).astype(BF16)
    for d in range(MP):
        part_ref[d] = part


def join_kernel(*refs):
    refs[-1][...] = jnp.concatenate([r[...] for r in refs[:-1]], axis=0)


def backward_kernel(*refs):
    shards, own_ref, t_ref, refs = refs[:MP], refs[MP], refs[MP + 1], refs[MP + 2:]
    part_ref, *qkv_ref, att_ref, scalar_ref, wo_ref = refs[:7]
    keep_ref, give_ref, grad_ref, turn_ref, text_ref, both_ref = refs[7:]
    me = lax.axis_index("dp")
    slot = lax.axis_index("mp")
    core = lax.rem(me, 2)
    pooled = jnp.zeros((IMG, D), F32)
    for s in range(MP):
        pooled = pooled + part_ref[s].astype(F32)
    scale = scalar_ref[0:1, :]
    image_inv = lax.rsqrt(jnp.sum(pooled * pooled, axis=-1, keepdims=True) + EPS)
    unit = pooled * image_inv
    text = jnp.concatenate([own_ref[...], t_ref[...]], axis=0)
    wide_text = text.astype(F32)
    square = pieces(wide_text * wide_text, 2)
    ones = jnp.ones((IMG, D), BF16)
    text_inv = lax.rsqrt(dot(ones, square[0], LAST) + dot(ones, square[1], LAST) + EPS)
    cosine = dot(jnp.concatenate(pieces(unit, 3), axis=0), text, LAST)
    cosine = (cosine[0:8] + cosine[8:16] + cosine[16:24]) * text_inv
    logits = scale * cosine + scalar_ref[1:2, :]
    image_row = lax.broadcasted_iota(jnp.int32, (IMG, TEXT), 0)
    own = lanes((IMG, TEXT)) == core * MP + image_row
    pair = scale * (jax.nn.sigmoid(logits) - jnp.where(own, 1.0, 0.0))
    unit_grad = dot(
        jnp.concatenate(pieces(pair * text_inv, 3), axis=0), text, (((1,), (0,)), ((), ()))
    )
    unit_grad = unit_grad[0:8] + unit_grad[8:16] + unit_grad[16:24]
    pooled_grad = (unit_grad - unit * jnp.sum(unit * unit_grad, axis=-1, keepdims=True)) * image_inv
    resid = (pooled_grad * (1.0 / TOK)).astype(BF16)
    column = lax.broadcasted_iota(jnp.int32, (TEXT, DP), 0)
    owner = lanes((TEXT, DP))
    step_x = lax.rem(lax.rem(lax.div(me, 2), 4) - lax.rem(lax.div(owner, 2), 4) + 4, 4)
    step_y = lax.rem(lax.div(me, 8) + lax.div(owner, 8), 2)
    place = step_x * 32 + step_y * 16 + lax.rem(owner, 2) * MP + slot
    chosen = jnp.where(column == place, 1.0, 0.0).astype(BF16)
    mine = dot(jnp.concatenate(pieces(pair, 3), axis=0), chosen, (((1,), (0,)), ((), ())))
    pair_high, pair_low = pieces(mine[0:8] + mine[8:16] + mine[16:24], 2)
    unit_high, unit_low = pieces(unit, 2)
    text_grad = dot(
        jnp.concatenate([pair_high, pair_high, pair_low], axis=0),
        jnp.concatenate([unit_high, unit_low, unit_high], axis=0),
        FIRST,
    )
    text_ref[...] = jnp.zeros_like(text_ref)
    for i in range(12):
        text_ref[pl.ds(i, DP, stride=16), :] = text_grad[0:DP, i * 128:(i + 1) * 128]
    attend = dot(resid, wo_ref[...], LAST).astype(BF16)
    wide_attend = attend.astype(F32)
    lane = lanes((64, WIDTH))
    slim = lanes((64, 64))
    for b in range(IMG):
        rows = slice(b * 64, (b + 1) * 64)
        q, k = qkv_ref[0][rows, 0:WIDTH], qkv_ref[1][rows, 0:WIDTH]
        product = qkv_ref[2][rows, 0:WIDTH].astype(F32) * wide_attend[b:b + 1, :]
        query_grad, key_grad, factor = [], [], jnp.zeros((64, 64), F32)
        for h in range(2):
            inside = lane < DH if h == 0 else lane >= DH
            prob_grad = jnp.sum(jnp.where(inside, product, 0.0), axis=1, keepdims=True)
            probs = qkv_ref[h][rows, WIDTH:256].astype(F32)
            mean = jnp.sum(probs * prob_grad, axis=0, keepdims=True)
            score_grad = (probs * (prob_grad - mean) * SCALE).astype(BF16)
            query_grad.append(dot(score_grad, k, FIRST))
            key_grad.append(dot(score_grad, q, (((1,), (0,)), ((), ()))))
            column = jnp.sum(probs, axis=1, keepdims=True)
            factor = factor + jnp.where(slim == h * 8 + b, column, 0.0)
        query_grad = jnp.where(lane < DH, query_grad[0], query_grad[1])
        key_grad = jnp.where(lane < DH, key_grad[0], key_grad[1])
        first = jnp.where(core == 0, factor, 0.0)
        full = jnp.concatenate([query_grad, first, key_grad, factor - first], axis=1)
        for s in range(MP):
            grad_ref[(s * 8 + b) * 8:(s * 8 + b) * 8 + 8, :] = full[s * 8:s * 8 + 8, :]
    turn_ref[...] = jnp.zeros_like(turn_ref)
    start = pl.multiple_of(core * 128, 128)
    for h in range(2):
        part = slice(h * DH, (h + 1) * DH)
        turn_ref[pl.ds(start + 96 + h * 8, 8), 0:DH] = wide_attend[:, part]
        turn_ref[pl.ds(start + 112 + h * 8, 8), 0:DH] = att_ref[:, part]
    turned = [turn_ref[i * 128:(i + 1) * 128, :].T[0:DH, :] for i in range(2)]
    place = lanes((IMG, 512)) - lax.broadcasted_iota(jnp.int32, (IMG, 512), 0) - core * 256
    spot = jnp.where((place == 208) | (place == 216), 1.0, 0.0).astype(BF16)
    normed = jnp.concatenate([r[0:64, :] for r in shards], axis=0)
    grads = grad_ref[...].astype(BF16)
    for c in range(4):
        columns = slice(c * 384, (c + 1) * 384)
        y = dot(normed[:, columns], grads, FIRST) + dot(resid[:, columns], spot, FIRST)
        for j in range(4):
            d = c * 4 + j
            for i in range(4):
                block = y[j * 96:(j + 1) * 96, i * 128:(i + 1) * 128]
                if i % 2 == 1:
                    block = block + turned[i // 2]
                both_ref[d % 2, d // 2, i * 96:(i + 1) * 96, :] = block.astype(BF16)
            both_ref[d % 2, d // 2, 384:400, :] = text_ref[d * 16:(d + 1) * 16, :].astype(BF16)
    keep_ref[...] = both_ref[core]
    give_ref[...] = both_ref[1 - core]


def finish_kernel(r_ref, text_ref, gain_ref, text_out, qkv_out, out_out, stack_ref, line_ref):
    total = r_ref[0].astype(F32)
    for s in range(1, 8):
        total = total + r_ref[s].astype(F32)
    unit_grad = total[384:396, :]
    for i in range(12):
        line_ref[i:i + 1, :] = text_ref[:, i * 128:(i + 1) * 128].astype(F32)
    text = line_ref[...]
    inv = lax.rsqrt(jnp.sum(text * text, keepdims=True) + EPS)
    unit = text * inv
    line_ref[...] = (unit_grad - unit * jnp.sum(unit * unit_grad, keepdims=True)) * inv
    for i in range(12):
        text_out[:, i * 128:(i + 1) * 128] = line_ref[i:i + 1, :]
    first = lax.axis_index("dp") * 96
    shift = lax.rem(first, 128)
    above = gain_ref[pl.ds(lax.div(first, 128), 1), :]
    below = gain_ref[pl.ds(jnp.minimum(lax.div(first, 128) + 1, 11), 1), :]
    gain = jnp.where(lanes((1, 128)) < shift, below, above)
    gain = pltpu.roll(gain, lax.rem(128 - shift, 128), axis=1)[:, 0:96]
    pad = jnp.zeros((32, 128), F32)
    for c in range(2):
        for i in range(2):
            at = (c * 2 + i) * 96
            turned = jnp.concatenate([total[at:at + 96, :], pad], axis=0).T
            rows = 128 if i == 0 else 64
            qkv_out[c, i * 128:i * 128 + rows, :] = turned[0:rows, 0:96] * gain
    lane = lanes((96, 128))
    group = lax.shift_right_logical(lane, 3) - 8
    factors = []
    for s in range(8):
        for c in range(2):
            block = r_ref[s, (c * 2 + 1) * 96:(c * 2 + 2) * 96, :]
            factors.append(block)
            rolled = pltpu.roll(block.astype(F32), 96, axis=1).astype(BF16)
            for g in range(4):
                at = (s * 2 + c) * 128
                stack_ref[g * 96:(g + 1) * 96, at:at + 128] = jnp.where(
                    group == g, rolled, jnp.zeros_like(rolled)
                )
    product = dot(stack_ref[...], jnp.concatenate(factors, axis=1), LAST)
    qkv_out[2] = product[0:192, :] * gain
    out_out[...] = product[192:384, :]


HERE = pl.BlockSpec(memory_space=pltpu.VMEM)
ANY = pl.BlockSpec(memory_space=pl.ANY)
SMEM = pl.BlockSpec(memory_space=pltpu.SMEM)


def call(kernel, outs, scratch, *args, specs=None, params=PARAMS):
    return pl.pallas_call(
        kernel,
        out_shape=[jax.ShapeDtypeStruct(*o) for o in outs],
        in_specs=specs or [HERE] * len(args),
        out_specs=[HERE] * len(outs),
        scratch_shapes=[pltpu.VMEM(*s) if isinstance(s, tuple) else s for s in scratch],
        compiler_params=params,
    )(*args)


def over_mp(block, dz, dy):
    route = [(i, ((i // 2 + dz) % 4) * 2 + (i % 2 + dy) % 2) for i in range(MP)]
    return lax.ppermute(block, "mp", route)


def over_dp(block, dy, dx, dc):
    route = [
        (i, ((i // 8 + dy) % 2 * 4 + (i // 2 + dx) % 4) * 2 + (i + dc) % 2) for i in range(DP)
    ]
    return lax.ppermute(block, "dp", route)


def first_step(block):
    far = over_mp(block, 2, 0)
    across, ahead, behind = [over_mp(block, dz, dy) for dz, dy in STEPS[1:4]]
    return [block, across, ahead, behind, far]


def second_step(blocks):
    across, far = blocks[1], blocks[4]
    return [over_mp(across, 1, 0), over_mp(across, 3, 0), over_mp(far, 0, 1)]


def body(tokens, norm_gain, qkv_weight, out_weight, text_embed, log_temp, logit_bias):
    own, token_sum = call(
        norm_kernel,
        [((72, D), BF16), ((IMG, D), F32)],
        [((12 * 64, 128), F32)],
        tokens,
    )
    own = lax.dynamic_update_slice(own, text_embed, (64, 0))
    own = lax.dynamic_update_slice(own, over_dp(text_embed, 0, 0, 1), (65, 0))
    shards = first_step(own)
    shards += second_step(shards)
    shards[2], log_temp, logit_bias = lax.optimization_barrier((shards[2], log_temp, logit_bias))
    scalars, = call(scalar_kernel, [((2, 128), F32)], [], log_temp, logit_bias, specs=[SMEM] * 2)
    shards[0], scalars = lax.optimization_barrier((shards[0], scalars))
    early, scaled = call(
        early_kernel,
        [((3, 320, WIDTH), BF16), ((3, WIDTH, D), BF16)],
        [((320, WIDTH), F32)],
        *shards[:5], qkv_weight, norm_gain.reshape(12, 128),
    )
    shards[0], early = lax.optimization_barrier((shards[0], early))
    kept, = call(
        functools.partial(text_kernel, 0, 7), [((16, D), F32)], [], *shards[:7],
        jnp.zeros((16, D), F32),
    )
    texts, = call(functools.partial(text_kernel, 7, 1), [((16, D), BF16)], [], shards[7], kept)
    texts = [texts, over_dp(texts, 1, 0, 0)]
    part, *qkv, attended = call(
        forward_kernel,
        [
            ((MP, IMG, D), BF16), ((512, 256), BF16), ((512, 256), BF16),
            ((512, WIDTH), BF16), ((IMG, WIDTH), F32),
        ],
        [((192, WIDTH), F32)],
        *shards[5:], early, scaled, out_weight, token_sum,
    )
    texts = jnp.concatenate(texts, axis=0)
    texts = [texts] + [over_dp(texts, 0, dx, 0) for dx in (1, 2, 3)]
    parts = lax.all_to_all(part, "mp", 0, 0)
    own_texts = texts[0]
    texts, = call(join_kernel, [((96, D), BF16)], [], *texts[1:])
    keep, give = call(
        backward_kernel,
        [((8, ROWS, 128), BF16)] * 2,
        [((512, 512), F32), ((256, 128), F32), ((256, 128), F32), ((2, 8, ROWS, 128), BF16)],
        *shards, own_texts, texts, parts, *qkv, attended, scalars, out_weight,
    )
    other = lax.ppermute(give, "dp", [(i, i ^ 1) for i in range(DP)])
    send = (keep.astype(F32) + other.astype(F32)).astype(BF16)
    received = lax.all_to_all(
        send, "dp", 0, 0, axis_index_groups=[list(range(c, DP, 2)) for c in range(2)]
    )
    text_grad, qkv_grad, out_grad = call(
        finish_kernel,
        [((1, D), F32), ((3, WIDTH, 96), F32), ((WIDTH, 96), F32)],
        [((384, 2048), BF16), ((12, 128), F32)],
        received, text_embed, norm_gain.reshape(12, 128),
    )
    return (text_grad, qkv_grad, out_grad)


def solution(mesh):
    placed = (
        P("dp", "mp"),
        P(),
        P(None, "mp", None),
        P("mp", None),
        P(("dp", "mp"), None),
        P(),
        P(),
    )
    return jax.shard_map(
        body,
        mesh=mesh,
        in_specs=placed,
        out_specs=(P(("dp", "mp"), None), P(None, "mp", "dp"), P("mp", "dp")),
        check_vma=False,
    )
```

```python
import functools
import math

import jax
import jax.numpy as jnp
from jax import lax
from jax.experimental import pallas as pl
from jax.experimental.pallas import tpu as pltpu
from jax.sharding import PartitionSpec as P

D = 1536
DH = 96
TOK = 64
IMG = 8
MP = 8
DP = 16
TEXT = DP * MP
WIDTH = 192
EPS = 1e-06
F32 = jnp.float32
BF16 = jnp.bfloat16
SCALE = 1.0 / math.sqrt(DH)
ROWS = 400
LAST = (((1,), (1,)), ((), ()))
FIRST = (((0,), (0,)), ((), ()))
PARAMS = pltpu.CompilerParams(vmem_limit_bytes=48 * 1024 * 1024)


def dot(a, b, dims):
    return lax.dot_general(a, b, dims, preferred_element_type=F32)


def pieces(a, n):
    out = []
    for _ in range(n):
        p = a.astype(BF16)
        out.append(p)
        a = a - p.astype(F32)
    return out


def lanes(shape):
    return lax.broadcasted_iota(jnp.int32, shape, len(shape) - 1)


def norm_kernel(tok_ref, out_ref, sum_ref, rows_ref):
    total = jnp.zeros((IMG, D), F32)
    for t in range(8):
        x = tok_ref[:, t * D:(t + 1) * D].astype(F32)
        center = x - jnp.mean(x, axis=-1, keepdims=True)
        spread = jnp.mean(center * center, axis=-1, keepdims=True)
        row = center * lax.rsqrt(spread + EPS)
        for i in range(12):
            rows_ref[pl.ds(i * 64 + t, IMG, stride=8), :] = row[:, i * 128:(i + 1) * 128]
        total = total + x
    sum_ref[...] = total
    out_ref[0:64, :] = jnp.concatenate(
        [rows_ref[i * 64:(i + 1) * 64, :] for i in range(12)], axis=1
    ).astype(BF16)
    out_ref[64:72, :] = jnp.zeros((8, D), BF16)


def scalar_kernel(temp_ref, bias_ref, scalar_ref):
    scalar_ref[0:1, :] = jnp.exp(jnp.full((1, 128), temp_ref[0], F32))
    scalar_ref[1:2, :] = jnp.full((1, 128), bias_ref[0], F32)


STEPS = ((0, 0), (0, 1), (1, 0), (3, 0), (2, 0), (1, 1), (3, 1), (2, 1))


def source(slot, step):
    dz, dy = STEPS[step]
    return lax.rem(lax.div(slot, 2) + 4 - dz, 4) * 2 + lax.rem(lax.rem(slot, 2) + dy, 2)


def text_kernel(first, count, *refs):
    shards, (kept_ref, out_ref) = refs[:count], refs[count:]
    slot = lax.axis_index("mp")
    core = lax.rem(lax.axis_index("dp"), 2)
    row = lax.broadcasted_iota(jnp.int32, (16, D), 0)
    total = kept_ref[...]
    for s in range(count):
        two = shards[s][64:72, :].astype(F32)
        for i in range(2):
            at = lax.rem(core + i, 2) * 8 + source(slot, first + s)
            total = jnp.where(row == at, two[i:i + 1, :], total)
    out_ref[...] = total.astype(out_ref.dtype)


def early_kernel(*refs):
    shards, (raw_ref, gain_ref, qkv_ref, w_ref, wide_ref) = refs[:5], refs[5:]
    for i in range(12):
        part = slice(i * 128, (i + 1) * 128)
        for c in range(3):
            scaled = raw_ref[c, :, part].astype(F32) * gain_ref[i:i + 1, :]
            w_ref[c, :, part] = scaled.astype(BF16)
    normed = jnp.concatenate([r[0:64, :] for r in shards], axis=0)
    for c in range(3):
        wide_ref[...] = dot(normed, w_ref[c], LAST)
        for b in range(IMG):
            block = jnp.concatenate(
                [wide_ref[(s * 8 + b) * 8:(s * 8 + b) * 8 + 8, :] for s in range(5)], axis=0
            )
            qkv_ref[c, b * 40:(b + 1) * 40, :] = block.astype(BF16)


def forward_kernel(*refs):
    shards, (early_ref, w_ref, wo_ref, sum_ref), refs = refs[:3], refs[3:7], refs[7:]
    part_ref, *qkv_ref, att_ref, wide_ref = refs
    normed = jnp.concatenate([r[0:64, :] for r in shards], axis=0)
    for c in range(3):
        wide_ref[...] = dot(normed, w_ref[c], LAST)
        for b in range(IMG):
            block = jnp.concatenate(
                [early_ref[c, b * 40:(b + 1) * 40, :].astype(F32)]
                + [wide_ref[(s * 8 + b) * 8:(s * 8 + b) * 8 + 8, :] for s in range(3)], axis=0
            )
            qkv_ref[c][b * 64:(b + 1) * 64, 0:WIDTH] = block.astype(BF16)
    lane = lanes((64, WIDTH))
    for b in range(IMG):
        rows = slice(b * 64, (b + 1) * 64)
        q, k = qkv_ref[0][rows, 0:WIDTH], qkv_ref[1][rows, 0:WIDTH]
        v = qkv_ref[2][rows, 0:WIDTH].astype(F32)
        columns = []
        for h in range(2):
            inside = lane < DH if h == 0 else lane >= DH
            score = dot(k, jnp.where(inside, q, jnp.zeros_like(q)), LAST) * SCALE
            weights = jnp.exp(score)
            probs = (weights / jnp.sum(weights, axis=0, keepdims=True)).astype(BF16)
            qkv_ref[h][rows, WIDTH:256] = probs
            columns.append(jnp.sum(probs.astype(F32), axis=1, keepdims=True))
        attended = jnp.sum(jnp.where(lane < DH, columns[0], columns[1]) * v, axis=0, keepdims=True)
        att_ref[b:b + 1, :] = attended
    high, low = pieces(att_ref[...], 2)
    branch = dot(jnp.concatenate([high, low], axis=0), wo_ref[...], (((1,), (0,)), ((), ())))
    part = ((branch[0:8] + branch[8:16] + sum_ref[...]) * (1.0 / TOK)).astype(BF16)
    for d in range(MP):
        part_ref[d] = part


def join_kernel(*refs):
    refs[-1][...] = jnp.concatenate([r[...] for r in refs[:-1]], axis=0)


def backward_kernel(*refs):
    shards, own_ref, t_ref, last_ref, refs = refs[:MP], *refs[MP:MP + 3], refs[MP + 3:]
    part_ref, *qkv_ref, att_ref, scalar_ref, wo_ref = refs[:7]
    keep_ref, give_ref, grad_ref, turn_ref, text_ref, both_ref = refs[7:]
    me = lax.axis_index("dp")
    slot = lax.axis_index("mp")
    core = lax.rem(me, 2)
    pooled = jnp.zeros((IMG, D), F32)
    for s in range(MP):
        pooled = pooled + part_ref[s].astype(F32)
    scale = scalar_ref[0:1, :]
    image_inv = lax.rsqrt(jnp.sum(pooled * pooled, axis=-1, keepdims=True) + EPS)
    unit = pooled * image_inv
    text = jnp.concatenate([own_ref[...], t_ref[...], last_ref[...]], axis=0)
    wide_text = text.astype(F32)
    square = pieces(wide_text * wide_text, 2)
    ones = jnp.ones((IMG, D), BF16)
    text_inv = lax.rsqrt(dot(ones, square[0], LAST) + dot(ones, square[1], LAST) + EPS)
    cosine = dot(jnp.concatenate(pieces(unit, 3), axis=0), text, LAST)
    cosine = (cosine[0:8] + cosine[8:16] + cosine[16:24]) * text_inv
    logits = scale * cosine + scalar_ref[1:2, :]
    image_row = lax.broadcasted_iota(jnp.int32, (IMG, TEXT), 0)
    own = lanes((IMG, TEXT)) == core * MP + image_row
    pair = scale * (jax.nn.sigmoid(logits) - jnp.where(own, 1.0, 0.0))
    unit_grad = dot(
        jnp.concatenate(pieces(pair * text_inv, 3), axis=0), text, (((1,), (0,)), ((), ()))
    )
    unit_grad = unit_grad[0:8] + unit_grad[8:16] + unit_grad[16:24]
    pooled_grad = (unit_grad - unit * jnp.sum(unit * unit_grad, axis=-1, keepdims=True)) * image_inv
    resid = (pooled_grad * (1.0 / TOK)).astype(BF16)
    column = lax.broadcasted_iota(jnp.int32, (TEXT, DP), 0)
    owner = lanes((TEXT, DP))
    step_x = lax.rem(lax.rem(lax.div(me, 2), 4) - lax.rem(lax.div(owner, 2), 4) + 4, 4)
    step_y = lax.rem(lax.div(me, 8) + lax.div(owner, 8), 2)
    place = step_x * 32 + step_y * 16 + lax.rem(owner, 2) * MP + slot
    chosen = jnp.where(column == place, 1.0, 0.0).astype(BF16)
    mine = dot(jnp.concatenate(pieces(pair, 3), axis=0), chosen, (((1,), (0,)), ((), ())))
    pair_high, pair_low = pieces(mine[0:8] + mine[8:16] + mine[16:24], 2)
    unit_high, unit_low = pieces(unit, 2)
    text_grad = dot(
        jnp.concatenate([pair_high, pair_high, pair_low], axis=0),
        jnp.concatenate([unit_high, unit_low, unit_high], axis=0),
        FIRST,
    )
    text_ref[...] = jnp.zeros_like(text_ref)
    for i in range(12):
        text_ref[pl.ds(i, DP, stride=16), :] = text_grad[0:DP, i * 128:(i + 1) * 128]
    attend = dot(resid, wo_ref[...], LAST).astype(BF16)
    wide_attend = attend.astype(F32)
    lane = lanes((64, WIDTH))
    slim = lanes((64, 64))
    for b in range(IMG):
        rows = slice(b * 64, (b + 1) * 64)
        q, k = qkv_ref[0][rows, 0:WIDTH], qkv_ref[1][rows, 0:WIDTH]
        product = qkv_ref[2][rows, 0:WIDTH].astype(F32) * wide_attend[b:b + 1, :]
        query_grad, key_grad, factor = [], [], jnp.zeros((64, 64), F32)
        for h in range(2):
            inside = lane < DH if h == 0 else lane >= DH
            prob_grad = jnp.sum(jnp.where(inside, product, 0.0), axis=1, keepdims=True)
            probs = qkv_ref[h][rows, WIDTH:256].astype(F32)
            mean = jnp.sum(probs * prob_grad, axis=0, keepdims=True)
            score_grad = (probs * (prob_grad - mean) * SCALE).astype(BF16)
            query_grad.append(dot(score_grad, k, FIRST))
            key_grad.append(dot(score_grad, q, (((1,), (0,)), ((), ()))))
            column = jnp.sum(probs, axis=1, keepdims=True)
            factor = factor + jnp.where(slim == h * 8 + b, column, 0.0)
        query_grad = jnp.where(lane < DH, query_grad[0], query_grad[1])
        key_grad = jnp.where(lane < DH, key_grad[0], key_grad[1])
        first = jnp.where(core == 0, factor, 0.0)
        full = jnp.concatenate([query_grad, first, key_grad, factor - first], axis=1)
        for s in range(MP):
            grad_ref[(s * 8 + b) * 8:(s * 8 + b) * 8 + 8, :] = full[s * 8:s * 8 + 8, :]
    turn_ref[...] = jnp.zeros_like(turn_ref)
    start = pl.multiple_of(core * 128, 128)
    for h in range(2):
        part = slice(h * DH, (h + 1) * DH)
        turn_ref[pl.ds(start + 96 + h * 8, 8), 0:DH] = wide_attend[:, part]
        turn_ref[pl.ds(start + 112 + h * 8, 8), 0:DH] = att_ref[:, part]
    turned = [turn_ref[i * 128:(i + 1) * 128, :].T[0:DH, :] for i in range(2)]
    place = lanes((IMG, 512)) - lax.broadcasted_iota(jnp.int32, (IMG, 512), 0) - core * 256
    spot = jnp.where((place == 208) | (place == 216), 1.0, 0.0).astype(BF16)
    normed = jnp.concatenate([r[0:64, :] for r in shards], axis=0)
    grads = grad_ref[...].astype(BF16)
    for c in range(4):
        columns = slice(c * 384, (c + 1) * 384)
        y = dot(normed[:, columns], grads, FIRST) + dot(resid[:, columns], spot, FIRST)
        for j in range(4):
            d = c * 4 + j
            for i in range(4):
                block = y[j * 96:(j + 1) * 96, i * 128:(i + 1) * 128]
                if i % 2 == 1:
                    block = block + turned[i // 2]
                both_ref[d % 2, d // 2, i * 96:(i + 1) * 96, :] = block.astype(BF16)
            both_ref[d % 2, d // 2, 384:400, :] = text_ref[d * 16:(d + 1) * 16, :].astype(BF16)
    keep_ref[...] = both_ref[core]
    give_ref[...] = both_ref[1 - core]


def finish_kernel(r_ref, text_ref, gain_ref, text_out, qkv_out, out_out, stack_ref, line_ref):
    total = r_ref[0].astype(F32)
    for s in range(1, 8):
        total = total + r_ref[s].astype(F32)
    unit_grad = total[384:396, :]
    for i in range(12):
        line_ref[i:i + 1, :] = text_ref[:, i * 128:(i + 1) * 128].astype(F32)
    text = line_ref[...]
    inv = lax.rsqrt(jnp.sum(text * text, keepdims=True) + EPS)
    unit = text * inv
    line_ref[...] = (unit_grad - unit * jnp.sum(unit * unit_grad, keepdims=True)) * inv
    for i in range(12):
        text_out[:, i * 128:(i + 1) * 128] = line_ref[i:i + 1, :]
    first = lax.axis_index("dp") * 96
    shift = lax.rem(first, 128)
    above = gain_ref[pl.ds(lax.div(first, 128), 1), :]
    below = gain_ref[pl.ds(jnp.minimum(lax.div(first, 128) + 1, 11), 1), :]
    gain = jnp.where(lanes((1, 128)) < shift, below, above)
    gain = pltpu.roll(gain, lax.rem(128 - shift, 128), axis=1)[:, 0:96]
    pad = jnp.zeros((32, 128), F32)
    for c in range(2):
        for i in range(2):
            at = (c * 2 + i) * 96
            turned = jnp.concatenate([total[at:at + 96, :], pad], axis=0).T
            rows = 128 if i == 0 else 64
            qkv_out[c, i * 128:i * 128 + rows, :] = turned[0:rows, 0:96] * gain
    lane = lanes((96, 128))
    group = lax.shift_right_logical(lane, 3) - 8
    factors = []
    for s in range(8):
        for c in range(2):
            block = r_ref[s, (c * 2 + 1) * 96:(c * 2 + 2) * 96, :]
            factors.append(block)
            rolled = pltpu.roll(block.astype(F32), 96, axis=1).astype(BF16)
            for g in range(4):
                at = (s * 2 + c) * 128
                stack_ref[g * 96:(g + 1) * 96, at:at + 128] = jnp.where(
                    group == g, rolled, jnp.zeros_like(rolled)
                )
    product = dot(stack_ref[...], jnp.concatenate(factors, axis=1), LAST)
    qkv_out[2] = product[0:192, :] * gain
    out_out[...] = product[192:384, :]


HERE = pl.BlockSpec(memory_space=pltpu.VMEM)
ANY = pl.BlockSpec(memory_space=pl.ANY)
SMEM = pl.BlockSpec(memory_space=pltpu.SMEM)


def call(kernel, outs, scratch, *args, specs=None, params=PARAMS):
    return pl.pallas_call(
        kernel,
        out_shape=[jax.ShapeDtypeStruct(*o) for o in outs],
        in_specs=specs or [HERE] * len(args),
        out_specs=[HERE] * len(outs),
        scratch_shapes=[pltpu.VMEM(*s) if isinstance(s, tuple) else s for s in scratch],
        compiler_params=params,
    )(*args)


def over_mp(block, dz, dy):
    route = [(i, ((i // 2 + dz) % 4) * 2 + (i % 2 + dy) % 2) for i in range(MP)]
    return lax.ppermute(block, "mp", route)


def over_dp(block, dy, dx, dc):
    route = [
        (i, ((i // 8 + dy) % 2 * 4 + (i // 2 + dx) % 4) * 2 + (i + dc) % 2) for i in range(DP)
    ]
    return lax.ppermute(block, "dp", route)


def first_step(block):
    far = over_mp(block, 2, 0)
    across, ahead, behind = [over_mp(block, dz, dy) for dz, dy in STEPS[1:4]]
    return [block, across, ahead, behind, far]


def second_step(blocks):
    across, far = blocks[1], blocks[4]
    return [over_mp(across, 1, 0), over_mp(across, 3, 0), over_mp(far, 0, 1)]


def body(tokens, norm_gain, qkv_weight, out_weight, text_embed, log_temp, logit_bias):
    own, token_sum = call(
        norm_kernel,
        [((72, D), BF16), ((IMG, D), F32)],
        [((12 * 64, 128), F32)],
        tokens,
    )
    own = lax.dynamic_update_slice(own, text_embed, (64, 0))
    own = lax.dynamic_update_slice(own, over_dp(text_embed, 0, 0, 1), (65, 0))
    shards = first_step(own)
    shards += second_step(shards)
    shards[2], log_temp, logit_bias = lax.optimization_barrier((shards[2], log_temp, logit_bias))
    scalars, = call(scalar_kernel, [((2, 128), F32)], [], log_temp, logit_bias, specs=[SMEM] * 2)
    shards[0], scalars = lax.optimization_barrier((shards[0], scalars))
    early, scaled = call(
        early_kernel,
        [((3, 320, WIDTH), BF16), ((3, WIDTH, D), BF16)],
        [((320, WIDTH), F32)],
        *shards[:5], qkv_weight, norm_gain.reshape(12, 128),
    )
    shards[0], early = lax.optimization_barrier((shards[0], early))
    kept, = call(
        functools.partial(text_kernel, 0, 7), [((16, D), F32)], [], *shards[:7],
        jnp.zeros((16, D), F32),
    )
    texts, = call(functools.partial(text_kernel, 7, 1), [((16, D), BF16)], [], shards[7], kept)
    texts = [texts, over_dp(texts, 1, 0, 0)]
    part, *qkv, attended = call(
        forward_kernel,
        [
            ((MP, IMG, D), BF16), ((512, 256), BF16), ((512, 256), BF16),
            ((512, WIDTH), BF16), ((IMG, WIDTH), F32),
        ],
        [((192, WIDTH), F32)],
        *shards[5:], early, scaled, out_weight, token_sum,
    )
    texts = jnp.concatenate(texts, axis=0)
    texts = [texts] + [over_dp(texts, 0, dx, 0) for dx in (1, 2, 3)]
    parts = lax.all_to_all(part, "mp", 0, 0)
    own_texts = texts[0]
    last_texts = texts[3]
    texts, = call(join_kernel, [((64, D), BF16)], [], *texts[1:3])
    keep, give = call(
        backward_kernel,
        [((8, ROWS, 128), BF16)] * 2,
        [((512, 512), F32), ((256, 128), F32), ((256, 128), F32), ((2, 8, ROWS, 128), BF16)],
        *shards, own_texts, texts, last_texts, parts, *qkv, attended, scalars, out_weight,
    )
    other = lax.ppermute(give, "dp", [(i, i ^ 1) for i in range(DP)])
    send = (keep.astype(F32) + other.astype(F32)).astype(BF16)
    received = lax.all_to_all(
        send, "dp", 0, 0, axis_index_groups=[list(range(c, DP, 2)) for c in range(2)]
    )
    text_grad, qkv_grad, out_grad = call(
        finish_kernel,
        [((1, D), F32), ((3, WIDTH, 96), F32), ((WIDTH, 96), F32)],
        [((384, 2048), BF16), ((12, 128), F32)],
        received, text_embed, norm_gain.reshape(12, 128),
    )
    return (text_grad, qkv_grad, out_grad)


def solution(mesh):
    placed = (
        P("dp", "mp"),
        P(),
        P(None, "mp", None),
        P("mp", None),
        P(("dp", "mp"), None),
        P(),
        P(),
    )
    return jax.shard_map(
        body,
        mesh=mesh,
        in_specs=placed,
        out_specs=(P(("dp", "mp"), None), P(None, "mp", "dp"), P("mp", "dp")),
        check_vma=False,
    )
```
